256 devices in a mesh: ctx: 32 (over z, x_hi, core), tp: 8 (over x_lo, y).
Axes of the slice: x: 4 (x_hi: 2, x_lo: 2; x = x_hi * 2 + x_lo), y: 4, z: 8, core: 2. Of those that a mesh axis runs over, the one named last changes fastest.
Arguments:
- query_proj: bfloat16 [16384, 4096], P('ctx', 'tp'), may hold values from -6 to 6
- key_proj: bfloat16 [16384, 4096], P('ctx', 'tp'), may hold values from -6 to 6
- value_proj: bfloat16 [16384, 4096], P('ctx', 'tp'), may hold values from -6 to 6
- cotangent: bfloat16 [16384, 4096], P('ctx', 'tp'), may hold values from -6 to 6
- out_weight: bfloat16 [4096, 4096], P('tp'), may hold values from -0.09375 to 0.09375
- decay_rates: float32 [4096, 16], P('tp'), may hold values from 3.0517578e-05 to 0.1
- residues: float32 [4096, 16], P('tp'), may hold values from -1.8 to 1.8
- skip_gain: float32 [4096], P('tp'), may hold values from 0.5 to 1.5
Outputs:
- mixed: bfloat16 [16384, 4096], P('ctx', 'tp')
- grad_query: bfloat16 [16384, 4096], P('ctx', 'tp')
- grad_key: bfloat16 [16384, 4096], P('ctx', 'tp')
- grad_value: bfloat16 [16384, 4096], P('ctx', 'tp')
The draws below stay inside these ranges and needn't reach their ends.
All inputs are finite; a program needn't handle non-finite values.
Results may differ from the reference program's by a relative error of at most 0.023.
Values may be sent and summed in bfloat16 or wider, within the bound.
No kernel may reach another device: no remote copies, remote signals or barrier semaphores. Data moves between devices by JAX's collectives and lax.ppermute only.
A program may use at most 64 MiB of HBM per device.

```python
import math
import jax
import jax.numpy as jnp
from jax import lax

D = 4096
STATE = 16
SEQ = 16384
N_TP = 8


def shard_levels(rng, extent, cuts, low, largest):
    gain = 1.0
    for axis_at, parts in cuts:
        steps = jax.random.uniform(jax.random.fold_in(jax.random.fold_in(rng, 6), axis_at), (parts,), jnp.float32, low / len(cuts), largest / len(cuts))
        gain = gain * jnp.repeat(jnp.exp(steps), extent[axis_at] // parts).reshape((-1,) + (1,) * (len(extent) - 1 - axis_at))
    return gain


def normal_values(key, shape, deviation, reach, cuts=(), held_as=jnp.bfloat16):
    values = deviation * jax.random.normal(key, shape, jnp.float32)
    if cuts:
        values = values * shard_levels(key, shape, cuts, -0.22, 0.18)
    return jnp.clip(values, -reach, reach).astype(held_as)


def setup_inputs(seed: int = 0) -> dict:
    keys = jax.random.split(jax.random.key(seed), 9)
    query_proj = normal_values(keys[0], (SEQ, D), 1.0, 6.0, ((0, 32), (1, 8)))
    key_proj = normal_values(keys[1], (SEQ, D), 1.0, 6.0, ((0, 32), (1, 8)))
    value_proj = normal_values(keys[2], (SEQ, D), 1.0, 6.0, ((0, 32), (1, 8)))
    cotangent = normal_values(keys[3], (SEQ, D), 1.0, 6.0, ((0, 32), (1, 8)))
    out_weight = normal_values(keys[4], (D, D), D ** -0.5, 0.09375, ((0, 8),))
    decay_rates = jnp.clip(jnp.exp(math.log(0.1) - 8.094623 * jax.random.uniform(keys[5], (D, STATE), jnp.float32) ** shard_levels(keys[5], (D, STATE), ((0, 8),), -0.2, 0.2)), 3.0517578125e-05, 0.1)
    residues = normal_values(keys[6], (D, STATE), 0.3, 1.8, ((0, 8),), jnp.float32)
    skip_gain = jnp.clip(0.5 + 1.0 * jax.random.uniform(keys[7], (D,), jnp.float32) ** shard_levels(keys[7], (D,), ((0, 8),), -0.2, 0.2), 0.5, 1.5)
    return {"query_proj": query_proj, "key_proj": key_proj, "value_proj": value_proj, "cotangent": cotangent, "out_weight": out_weight, "decay_rates": decay_rates, "residues": residues, "skip_gain": skip_gain}


block_len = 128
highest = lax.Precision.HIGHEST

def pair_combine(earlier, later):
    return (earlier[0] * later[0], earlier[1] * later[0] + later[1])

def amplitude_of(decay_rates, residues):
    return residues * jnp.sqrt(-jnp.expm1(-2.0 * decay_rates))

def toeplitz_table(decay_rates, residues):
    steps_f = jnp.arange(block_len).astype(jnp.float32)
    amplitude = amplitude_of(decay_rates, residues)
    falling = amplitude[:, :, None] * jnp.exp(-decay_rates[:, :, None] * steps_f)
    rising = jnp.exp(decay_rates[:, :, None] * steps_f)
    table = jnp.einsum('cmi,cmj->cij', falling, rising, precision=highest)
    below = steps_f[:, None] >= steps_f[None, :]
    return jnp.where(below[None], table, 0.0)

def tail_table(decay_rates):
    steps_f = jnp.arange(block_len).astype(jnp.float32)
    return jnp.exp(-decay_rates[:, :, None] * (block_len - 1.0 - steps_f))

def head_table(decay_rates, residues):
    steps_f = jnp.arange(block_len).astype(jnp.float32)
    amplitude = amplitude_of(decay_rates, residues)
    return amplitude[:, :, None] * jnp.exp(-decay_rates[:, :, None] * (steps_f + 1.0))

def local_pass(signal, toeplitz, tails, decay_rates):
    channels, length = signal.shape
    blocks = signal.reshape(channels, length // block_len, block_len)
    inside = jnp.einsum('cij,cnj->cni', toeplitz, blocks, precision=highest)
    ends = jnp.einsum('cmj,cnj->nmc', tails, blocks, precision=highest)
    factor = jnp.broadcast_to(jnp.exp(-decay_rates * block_len).T[None], ends.shape)
    _, states = lax.associative_scan(pair_combine, (factor, ends), axis=0)
    return (inside, states)

def grouped_local(signal, decay_rates, residues):
    channels, length = signal.shape
    group_width = math.gcd(64, channels)
    group_count = channels // group_width

    def one_group(operands):
        part_data, part_rates, part_res = operands
        return local_pass(part_data, toeplitz_table(part_rates, part_res), tail_table(part_rates), part_rates)
    inside, states = lax.map(one_group, (signal.reshape(group_count, group_width, length), decay_rates.reshape(group_count, group_width, -1), residues.reshape(group_count, group_width, -1)))
    count = length // block_len
    states = jnp.transpose(states, (1, 2, 0, 3)).reshape(count, states.shape[2], channels)
    return (inside.reshape(channels, count, block_len), states)

def finish(inside, states, initial, heads, decay_rates):
    channels, count, _ = inside.shape
    before = jnp.concatenate([jnp.zeros_like(states[:1]), states[:-1]], axis=0)
    starts = (jnp.arange(count) * block_len).astype(jnp.float32)
    before = before + jnp.exp(-decay_rates.T[None, :, :] * starts[:, None, None]) * initial[None, :, :]
    across = jnp.einsum('cmi,nmc->cni', heads, before, precision=highest)
    return (inside + across).reshape(channels, count * block_len)

def long_conv(signal, decay_rates, residues, flipped):
    data = signal.astype(jnp.float32).T
    if flipped:
        data = data[:, ::-1]
    inside, states = grouped_local(data, decay_rates, residues)
    initial = jnp.zeros_like(states[0])
    result = finish(inside, states, initial, head_table(decay_rates, residues), decay_rates)
    if flipped:
        result = result[:, ::-1]
    return result.astype(jnp.bfloat16).T

def reference(query_proj, key_proj, value_proj, cotangent, out_weight, decay_rates, residues, skip_gain):
    gated = (key_proj.astype(jnp.float32) * value_proj.astype(jnp.float32)).astype(jnp.bfloat16)
    conv_out = long_conv(gated, decay_rates, residues, False)
    summed = conv_out.astype(jnp.float32) + skip_gain[None, :] * gated.astype(jnp.float32)
    output_in = (query_proj.astype(jnp.float32) * summed).astype(jnp.bfloat16)
    shard_cols = D // N_TP
    running = jnp.zeros((SEQ, D), jnp.float32)
    for shard_index in range(N_TP):
        lower = shard_index * shard_cols
        partial_value = jnp.dot(output_in[:, lower:lower + shard_cols], out_weight[lower:lower + shard_cols], preferred_element_type=jnp.float32).astype(jnp.bfloat16)
        running = running + lax.optimization_barrier(partial_value).astype(jnp.float32)
    mixed = running.astype(jnp.bfloat16)
    grad_in = jnp.dot(cotangent, out_weight.T, preferred_element_type=jnp.float32)
    grad_query = (grad_in * summed).astype(jnp.bfloat16)
    grad_conv = (grad_in * query_proj.astype(jnp.float32)).astype(jnp.bfloat16)
    back = long_conv(grad_conv, decay_rates, residues, True)
    grad_gated = back.astype(jnp.float32) + skip_gain[None, :] * grad_conv.astype(jnp.float32)
    grad_key = (grad_gated * value_proj.astype(jnp.float32)).astype(jnp.bfloat16)
    grad_value = (grad_gated * key_proj.astype(jnp.float32)).astype(jnp.bfloat16)
    return (mixed, grad_query, grad_key, grad_value)
```

```python
import jax
import jax.numpy as jnp
from jax import lax
from jax.experimental import pallas as pl
from jax.experimental.pallas import tpu as pltpu
from jax.sharding import PartitionSpec as P

F32, BF16 = jnp.float32, jnp.bfloat16
ROWS, COLS, MODES, LANES = 512, 512, 16, 128
HALF = ROWS // 2
TILES = COLS // LANES
PARTS = 8
STEP = ROWS // PARTS
VMEM = pl.BlockSpec(memory_space=pltpu.VMEM)
SMEM = pl.BlockSpec(memory_space=pltpu.SMEM)


def tile_of(tile):
    return slice(tile * LANES, (tile + 1) * LANES)


def spread(ref, tile, mode):
    return jnp.broadcast_to(ref[tile, mode : mode + 1, :], (PARTS, LANES))


def ends_of(signal, ends, keep, tile, flipped):
    decay = [spread(keep, tile, m) for m in range(MODES)]

    def step(i, states):
        at = STEP - 1 - i if flipped else i
        u = signal[tile, pl.ds(at, PARTS, stride=STEP), :]
        return tuple(decay[m] * states[m] + u for m in range(MODES))

    zero = jnp.zeros((PARTS, LANES), F32)
    states = lax.fori_loop(0, STEP, step, (zero,) * MODES, unroll=4)
    for m in range(MODES):
        ends[tile, pl.ds(m, PARTS, stride=MODES), :] = states[m]


def chain(ends, starts, total, keep_piece, tile, flipped):
    state = jnp.zeros((MODES, LANES), F32)
    factor = keep_piece[tile]
    order = range(PARTS - 1, -1, -1) if flipped else range(PARTS)
    for piece in order:
        rows = slice(piece * MODES, (piece + 1) * MODES)
        starts[tile, rows, :] = state
        state = factor * state + ends[tile, rows, :]
    total[tile] = state


def whole_starts(starts, initial, begin, keep_piece, tile, flipped):
    carried = initial[tile]
    factor = keep_piece[tile]
    order = range(PARTS - 1, -1, -1) if flipped else range(PARTS)
    for piece in order:
        rows = slice(piece * MODES, (piece + 1) * MODES)
        begin[tile, rows, :] = starts[tile, rows, :] + carried
        carried = factor * carried


def responses(signal, begin, result, keep, gain, tile, flipped):
    decay = [spread(keep, tile, m) for m in range(MODES)]
    gains = [spread(gain, tile, m) for m in range(MODES)]

    def step(i, states):
        at = STEP - 1 - i if flipped else i
        u = signal[tile, pl.ds(at, PARTS, stride=STEP), :]
        states = tuple(decay[m] * states[m] + u for m in range(MODES))
        terms = [gains[m] * states[m] for m in range(MODES)]
        while len(terms) > 1:
            terms = [terms[i] + terms[i + 1] for i in range(0, len(terms), 2)]
        result[tile, pl.ds(at, PARTS, stride=STEP), :] = terms[0]
        return states

    states = tuple(begin[tile, pl.ds(m, PARTS, stride=MODES), :] for m in range(MODES))
    lax.fori_loop(0, STEP, step, states, unroll=4)


def columns(weight, place, which):
    return weight[:, pl.ds(pl.multiple_of(place[which] * COLS, COLS), COLS)]


def dot(a, b):
    return jnp.dot(a, b, preferred_element_type=F32)


def wide(value):
    return value.astype(F32)


NEAR = [(0, 0), (1, 0), (0, -1), (0, 1), (1, -1), (1, 1), (0, 2), (1, 2)]
OWN, ACROSS, BELOW, ABOVE, ACROSS_BELOW, ACROSS_ABOVE, FAR, ACROSS_FAR = range(8)
TOP, BOTTOM = slice(0, HALF), slice(HALF, ROWS)


def gate_kernel(key, value, keep, keep_piece, gated, starts, total, signal, ends):
    for tile in range(TILES):
        lanes = tile_of(tile)
        product = (wide(key[:, lanes]) * wide(value[:, lanes])).astype(BF16)
        gated[:, lanes] = product
        signal[tile] = wide(product)
        ends_of(signal, ends, keep, tile, False)
        chain(ends, starts, total, keep_piece, tile, False)


def mix_kernel(
    place, gated, starts, initial, keep, keep_piece, gain, skip, query, weight,
    summed, mixed_in, far_t, far_b, above_b, below_t, two_t, two_b,
    signal, begin, result,
):
    for tile in range(TILES):
        lanes = tile_of(tile)
        signal[tile] = wide(gated[:, lanes])
        whole_starts(starts, initial, begin, keep_piece, tile, False)
        responses(signal, begin, result, keep, gain, tile, False)
        conv = wide(result[tile].astype(BF16))
        total = conv + skip[0:1, lanes] * signal[tile]
        summed[:, lanes] = total
        mixed_in[:, lanes] = (wide(query[:, lanes]) * total).astype(BF16)
    sends = (
        (far_t, ACROSS_FAR, TOP), (far_b, ACROSS_FAR, BOTTOM),
        (above_b, ACROSS_ABOVE, BOTTOM), (below_t, ACROSS_BELOW, TOP),
        (two_t, FAR, TOP), (two_b, FAR, BOTTOM),
    )
    for out, which, rows in sends:
        out[...] = dot(mixed_in[rows, :], columns(weight, place, which)).astype(BF16)


def second_kernel(place, mixed_in, weight, got_t, got_b, out_t, out_b):
    top = dot(mixed_in[TOP, :], columns(weight, place, ACROSS_ABOVE))
    out_t[...] = (top + wide(got_t[...])).astype(BF16)
    bottom = dot(mixed_in[BOTTOM, :], columns(weight, place, ACROSS_BELOW))
    out_b[...] = (bottom + wide(got_b[...])).astype(BF16)


def third_kernel(place, mixed_in, weight, x_t, x_b, p_t, p_b, m_t, m_b, out_x, out_p, out_m):
    trios = ((out_x, ACROSS, x_t, x_b), (out_p, ABOVE, p_t, p_b), (out_m, BELOW, m_t, m_b))
    for out, which, got_t, got_b in trios:
        for rows, got in ((TOP, got_t), (BOTTOM, got_b)):
            part = dot(mixed_in[rows, :], columns(weight, place, which))
            out[rows, :] = (part + wide(got[...])).astype(BF16)


def last_kernel(place, mixed_in, weight, x, p, m, out):
    for rows in (TOP, BOTTOM):
        part = dot(mixed_in[rows, :], columns(weight, place, OWN))
        part = part + wide(x[rows, :]) + (wide(p[rows, :]) + wide(m[rows, :]))
        out[rows, :] = part.astype(BF16)


def grad_kernel(
    place, weight, own, across, below, above, ab_t, ab_b, aa_t, aa_b, far_t, far_b, af_t, af_b,
    summed, query, keep, keep_piece,
    grad_query, grad_conv, starts, total,
    acc, signal, ends,
):
    wholes = ((own, OWN), (across, ACROSS), (below, BELOW), (above, ABOVE))
    halves = {
        TOP.start: ((ab_t, ACROSS_BELOW), (aa_t, ACROSS_ABOVE), (far_t, FAR), (af_t, ACROSS_FAR)),
        BOTTOM.start: ((ab_b, ACROSS_BELOW), (aa_b, ACROSS_ABOVE), (far_b, FAR), (af_b, ACROSS_FAR)),
    }
    turned = (((1,), (1,)), ((), ()))
    for rows in (TOP, BOTTOM):
        grad = jnp.zeros((HALF, COLS), F32)
        for ref, which in wholes:
            grad += lax.dot_general(
                ref[rows, :], columns(weight, place, which), turned, preferred_element_type=F32
            )
        for ref, which in halves[rows.start]:
            grad += lax.dot_general(
                ref[...], columns(weight, place, which), turned, preferred_element_type=F32
            )
        acc[rows, :] = grad
    for tile in range(TILES):
        lanes = tile_of(tile)
        grad = acc[:, lanes]
        grad_query[:, lanes] = (grad * summed[:, lanes]).astype(BF16)
        conv = (grad * wide(query[:, lanes])).astype(BF16)
        grad_conv[:, lanes] = conv
        signal[tile] = wide(conv)
        ends_of(signal, ends, keep, tile, True)
        chain(ends, starts, total, keep_piece, tile, True)


def back_kernel(
    grad_conv, starts, initial, keep, keep_piece, gain, skip, key, value,
    grad_key, grad_value,
    signal, begin, result,
):
    for tile in range(TILES):
        lanes = tile_of(tile)
        signal[tile] = wide(grad_conv[:, lanes])
        whole_starts(starts, initial, begin, keep_piece, tile, True)
        responses(signal, begin, result, keep, gain, tile, True)
        back = wide(result[tile].astype(BF16))
        total = back + skip[0:1, lanes] * signal[tile]
        grad_key[:, lanes] = (total * wide(value[:, lanes])).astype(BF16)
        grad_value[:, lanes] = (total * wide(key[:, lanes])).astype(BF16)


def call(kernel, outs, scratch, specs, flops, moved, *args):
    return pl.pallas_call(
        kernel,
        out_shape=[jax.ShapeDtypeStruct(shape, kind) for shape, kind in outs],
        in_specs=specs,
        out_specs=[VMEM] * len(outs),
        scratch_shapes=scratch,
        cost_estimate=pl.CostEstimate(flops=flops, bytes_accessed=moved, transcendentals=0),
        compiler_params=pltpu.CompilerParams(vmem_limit_bytes=24 * 1024 * 1024),
    )(*args)


def tp_perm(move):
    return [(x * 4 + y, move(x, y)[0] % 2 * 4 + move(x, y)[1] % 4) for x in range(2) for y in range(4)]


def ctx_perm(move):
    pairs = []
    for z in range(8):
        for h in range(2):
            for c in range(2):
                to = move(z, h, c)
                pairs.append((z * 4 + h * 2 + c, to[0] % 8 * 4 + to[1] % 2 * 2 + to[2] % 2))
    return pairs


def shift_x(value):
    return lax.ppermute(value, "tp", tp_perm(lambda x, y: (x + 1, y)))


def shift_up(value):
    return lax.ppermute(value, "tp", tp_perm(lambda x, y: (x, y + 1)))


def shift_down(value):
    return lax.ppermute(value, "tp", tp_perm(lambda x, y: (x, y + 3)))


def carried_in(own, rates, flipped):
    place = lax.axis_index("ctx")
    core, high, z = place % 2, place // 2 % 2, place // 4
    if flipped:
        core, high, z = 1 - core, 1 - high, 7 - z

    def power(n):
        return jnp.exp(rates * (-float(ROWS) * n.astype(F32)))

    other = lax.ppermute(own, "ctx", ctx_perm(lambda z, h, c: (z, h, c + 1)))
    pair = power(1 - core) * own + power(core) * other
    before = jnp.where(core == 1, other, 0.0)
    other = lax.ppermute(pair, "ctx", ctx_perm(lambda z, h, c: (z, h + 1, c)))
    group = power(2 - 2 * high) * pair + power(2 * high) * other
    before = before + jnp.where(high == 1, power(core) * other, 0.0)
    window, over = group, None
    for k in (1, 2, 4):
        move = -k if flipped else k
        other = lax.ppermute(window, "ctx", ctx_perm(lambda z, h, c: (z + move, h, c)))
        other = jnp.where(z >= k, other, 0.0)
        term = power(jnp.asarray(4 * (k - 1))) * other
        over = other if over is None else over + term
        if k < 4:
            window = window + power(jnp.asarray(4 * k)) * other
    return before + power(2 * high + core) * over


def per_device(query, key, value, cotangent, weight, decay_rates, residues, skip_gain):
    at = lax.axis_index("tp")
    x, y = at // 4, at % 4
    place = jnp.stack([(x + dx) % 2 * 4 + (y + dy + 4) % 4 for dx, dy in NEAR]).astype(jnp.int32)

    def by_tile(table):
        return table.reshape(TILES, LANES, MODES).transpose(0, 2, 1)

    rates = by_tile(decay_rates)
    keep, keep_piece = jnp.exp(-rates), jnp.exp(rates * -float(STEP))
    gain = by_tile(residues) * jnp.sqrt(-jnp.expm1(-2.0 * rates))
    skip = skip_gain.reshape(1, COLS)

    across = shift_x(cotangent)
    below = shift_up(cotangent)
    above = shift_down(cotangent)
    ab_t = shift_up(across[TOP])
    aa_b = shift_down(across[BOTTOM])
    ab_b = shift_x(below[BOTTOM])
    aa_t = shift_x(above[TOP])
    far_t = shift_up(below[TOP])
    far_b = shift_down(above[BOTTOM])
    af_t = shift_up(ab_t)
    af_b = shift_down(aa_b)

    state, block, half = (TILES, MODES, LANES), (ROWS, COLS), (HALF, COLS)
    table = (TILES, PARTS * MODES, LANES)
    deep = pltpu.VMEM((TILES, ROWS, LANES), F32)
    ends = pltpu.VMEM(table, F32)
    elements = ROWS * COLS
    local, product = 40 * elements, 2 * ROWS * COLS * COLS
    gated, starts, total = call(
        gate_kernel,
        [(block, BF16), (table, F32), (state, F32)],
        [deep, ends],
        [VMEM] * 4,
        local,
        6 * elements,
        key,
        value,
        keep,
        keep_piece,
    )
    initial = carried_in(total, rates, False)
    summed, mixed_in, s_far_t, s_far_b, s_above_b, s_below_t, s_two_t, s_two_b = call(
        mix_kernel,
        [(block, F32), (block, BF16)] + [(half, BF16)] * 6,
        [deep, ends, deep],
        [SMEM] + [VMEM] * 9,
        2 * local + 3 * product,
        16 * elements,
        place,
        gated,
        starts,
        initial,
        keep,
        keep_piece,
        gain,
        skip,
        query,
        weight,
    )
    g_above_t, g_below_b = shift_up(s_far_t), shift_down(s_far_b)
    g_p_b, g_m_t = shift_x(s_above_b), shift_x(s_below_t)
    g_p_t, g_m_b = shift_up(s_two_t), shift_down(s_two_b)

    grad_query, grad_conv, back_starts, back_total = call(
        grad_kernel,
        [(block, BF16), (block, BF16), (table, F32), (state, F32)],
        [pltpu.VMEM(block, F32), deep, ends],
        [SMEM] + [VMEM] * 17,
        local + 8 * product,
        32 * elements,
        place,
        weight,
        cotangent,
        across,
        below,
        above,
        ab_t,
        ab_b,
        aa_t,
        aa_b,
        far_t,
        far_b,
        af_t,
        af_b,
        summed,
        query,
        keep,
        keep_piece,
    )
    back_initial = carried_in(back_total, rates, True)

    s_x_t, s_x_b = call(
        second_kernel,
        [(half, BF16)] * 2,
        [],
        [SMEM] + [VMEM] * 4,
        product,
        6 * elements,
        place,
        mixed_in,
        weight,
        g_above_t,
        g_below_b,
    )
    g_x_t, g_x_b = shift_up(s_x_t), shift_down(s_x_b)
    s_x, s_p, s_m = call(
        third_kernel,
        [(block, BF16)] * 3,
        [],
        [SMEM] + [VMEM] * 8,
        3 * product,
        10 * elements,
        place,
        mixed_in,
        weight,
        g_x_t,
        g_x_b,
        g_p_t,
        g_p_b,
        g_m_t,
        g_m_b,
    )
    (mixed,) = call(
        last_kernel,
        [(block, BF16)],
        [],
        [SMEM] + [VMEM] * 5,
        product,
        8 * elements,
        place,
        mixed_in,
        weight,
        shift_x(s_x),
        shift_up(s_p),
        shift_down(s_m),
    )
    grad_key, grad_value = call(
        back_kernel,
        [(block, BF16), (block, BF16)],
        [deep, ends, deep],
        [VMEM] * 9,
        2 * local,
        12 * elements,
        grad_conv,
        back_starts,
        back_initial,
        keep,
        keep_piece,
        gain,
        skip,
        key,
        value,
    )
    return mixed, grad_query, grad_key, grad_value


def solution(mesh):
    split, rows = P("ctx", "tp"), P("tp", None)
    return jax.shard_map(
        per_device,
        mesh=mesh,
        in_specs=(split, split, split, split, rows, rows, rows, P("tp")),
        out_specs=(split, split, split, split),
        check_vma=False,
    )
```

```python
import functools

import jax
import jax.numpy as jnp
from jax import lax
from jax.experimental import pallas as pl
from jax.experimental.pallas import tpu as pltpu
from jax.sharding import PartitionSpec as P

F32, BF16 = jnp.float32, jnp.bfloat16
ROWS, COLS, MODES, LANES = 512, 512, 16, 128
HALF = ROWS // 2
TILES = COLS // LANES
PARTS = 8
STEP = ROWS // PARTS
VMEM = pl.BlockSpec(memory_space=pltpu.VMEM)
SMEM = pl.BlockSpec(memory_space=pltpu.SMEM)


def tile_of(tile):
    return slice(tile * LANES, (tile + 1) * LANES)


def spread(ref, tile, mode):
    return jnp.broadcast_to(ref[tile, mode : mode + 1, :], (PARTS, LANES))


def ends_of(signal, ends, keep, tile, flipped):
    decay = [spread(keep, tile, m) for m in range(MODES)]

    def step(i, states):
        at = STEP - 1 - i if flipped else i
        u = signal[tile, pl.ds(at, PARTS, stride=STEP), :]
        return tuple(decay[m] * states[m] + u for m in range(MODES))

    zero = jnp.zeros((PARTS, LANES), F32)
    states = lax.fori_loop(0, STEP, step, (zero,) * MODES, unroll=4)
    for m in range(MODES):
        ends[tile, pl.ds(m, PARTS, stride=MODES), :] = states[m]


def chain(ends, starts, total, keep_piece, tile, flipped):
    state = jnp.zeros((MODES, LANES), F32)
    factor = keep_piece[tile]
    order = range(PARTS - 1, -1, -1) if flipped else range(PARTS)
    for piece in order:
        rows = slice(piece * MODES, (piece + 1) * MODES)
        starts[tile, rows, :] = state
        state = factor * state + ends[tile, rows, :]
    total[tile] = state


def whole_starts(starts, initial, begin, keep_piece, tile, flipped):
    carried = initial
    factor = keep_piece[tile]
    order = range(PARTS - 1, -1, -1) if flipped else range(PARTS)
    for piece in order:
        rows = slice(piece * MODES, (piece + 1) * MODES)
        begin[tile, rows, :] = starts[tile, rows, :] + carried
        carried = factor * carried


def responses(signal, begin, result, keep, gain, tile, flipped):
    decay = [spread(keep, tile, m) for m in range(MODES)]
    gains = [spread(gain, tile, m) for m in range(MODES)]

    def step(i, states):
        at = STEP - 1 - i if flipped else i
        u = signal[tile, pl.ds(at, PARTS, stride=STEP), :]
        states = tuple(decay[m] * states[m] + u for m in range(MODES))
        terms = [gains[m] * states[m] for m in range(MODES)]
        while len(terms) > 1:
            terms = [terms[i] + terms[i + 1] for i in range(0, len(terms), 2)]
        result[tile, pl.ds(at, PARTS, stride=STEP), :] = terms[0]
        return states

    states = tuple(begin[tile, pl.ds(m, PARTS, stride=MODES), :] for m in range(MODES))
    lax.fori_loop(0, STEP, step, states, unroll=4)


def dot(a, b):
    return jnp.dot(a, b, preferred_element_type=F32)


def turned(a, b):
    return lax.dot_general(a, b, (((1,), (1,)), ((), ())), preferred_element_type=F32)


def wide(value):
    return value.astype(F32)


def columns(weight, place, which):
    return weight[:, pl.ds(pl.multiple_of(place[which] * COLS, COLS), COLS)]


NEAR = [(0, 0), (1, 0), (0, -1), (0, 1), (1, -1), (1, 1), (0, 2), (1, 2)]
OWN, ACROSS, BELOW, ABOVE, ACROSS_BELOW, ACROSS_ABOVE, FAR, ACROSS_FAR = range(8)
TOP, BOTTOM = slice(0, HALF), slice(HALF, ROWS)
PER_TILE = range(TILES)


def gate_kernel(
    spot, place, gated, decay_rates, amplitude, rates, keep, keep_piece, gain, starts, total, signal, ends,
):
    for tile in PER_TILE:
        at = tile_of(tile)
        rates[tile] = decay_rates[:, at]
        gain[tile] = amplitude[:, at]
        keep[tile] = jnp.exp(-rates[tile])
        keep_piece[tile] = jnp.exp(rates[tile] * -float(STEP))
        signal[tile] = wide(gated[:, at])
        ends_of(signal, ends, keep, tile, False)
        chain(ends, starts, total, keep_piece, tile, False)


def power(rates, n):
    return jnp.exp(rates * (-float(ROWS) * jnp.asarray(n).astype(F32)))


def spot_of(spot, flipped):
    core, high, z = spot[0], spot[1], spot[2]
    return (1 - core, 1 - high, 7 - z) if flipped else (core, high, z)


def pair_kernel(flipped, spot, rates, own, other, pair, before):
    core, _, _ = spot_of(spot, flipped)
    pair[...] = power(rates[...], 1 - core) * own[...] + power(rates[...], core) * other[...]
    before[...] = core.astype(F32) * other[...]


def three_kernel(flipped, spot, rates, pair, one_off, two_off, two, three):
    _, _, z = spot_of(spot, flipped)
    here = (z >= 1).astype(F32) * one_off[...]
    here += (z >= 2).astype(F32) * (power(rates[...], 4) * two_off[...])
    two[...] = here
    three[...] = pair[...] + power(rates[...], 4) * here


def over_of(rates, z, two, three_off, six_off):
    here = two + (z >= 3).astype(F32) * (power(rates, 8) * three_off)
    return here + (z >= 6).astype(F32) * (power(rates, 20) * six_off)


def sent_kernel(flipped, spot, rates, pair, two, three_off, six_off, after, over, sent):
    _, high, z = spot_of(spot, flipped)
    here = over_of(rates[...], z, two[...], three_off[...], six_off[...])
    over[...] = here
    later = high.astype(F32)
    sent[...] = later * here + (1.0 - later) * (pair[...] + power(rates[...], 4) * here)


def group_kernel(flipped, spot, rates, pair, before, other, group, before_all):
    core, high, _ = spot_of(spot, flipped)
    early, late = power(rates[...], 2 - 2 * high), power(rates[...], 2 * high)
    group[...] = early * pair[...] + late * other[...]
    before_all[...] = before[...] + high.astype(F32) * (power(rates[...], core) * other[...])


def pack_kernel(across, below, above, after, up, down, over):
    up[TOP, :], up[BOTTOM, :] = across[TOP, :], below[TOP, :]
    down[TOP, :], down[BOTTOM, :] = across[BOTTOM, :], above[BOTTOM, :]
    over[TOP, :], over[BOTTOM, :] = below[BOTTOM, :], above[TOP, :]


def halve_kernel(up, down, after, far_t, far_b):
    far_t[...] = up[TOP, :]
    far_b[...] = down[TOP, :]


def mix_kernel(
    spot, rates, other, over, before,
    gated, starts, keep, keep_piece, gain, skip, query, after_t, after_b,
    summed, mixed_in,
    signal, result, begin,
):
    for tile in PER_TILE:
        at = tile_of(tile)
        signal[tile] = wide(gated[:, at])
        core, _, _ = spot_of(spot, False)
        initial = other[tile] + power(rates[tile], 2) * over[tile]
        initial = power(rates[tile], core) * initial + before[tile]
        whole_starts(starts, initial, begin, keep_piece, tile, False)
        responses(signal, begin, result, keep, gain, tile, False)
        conv = wide(result[tile].astype(BF16))
        total = conv + skip[0:1, at] * signal[tile]
        summed[:, at] = total
        mixed_in[:, at] = (wide(query[:, at]) * total).astype(BF16)


def first_kernel(place, mixed_in, weight, after_t, after_b, up, down, over):
    top, bottom = mixed_in[TOP, :], mixed_in[BOTTOM, :]
    up[TOP, :] = dot(top, columns(weight, place, ACROSS_FAR)).astype(BF16)
    down[TOP, :] = dot(bottom, columns(weight, place, ACROSS_FAR)).astype(BF16)
    up[BOTTOM, :] = dot(top, columns(weight, place, FAR)).astype(BF16)
    down[BOTTOM, :] = dot(bottom, columns(weight, place, FAR)).astype(BF16)
    over[TOP, :] = dot(bottom, columns(weight, place, ACROSS_ABOVE)).astype(BF16)
    over[BOTTOM, :] = dot(top, columns(weight, place, ACROSS_BELOW)).astype(BF16)


def rest_kernel(place, mixed_in, weight, after, side, above, below, across, own):
    top, bottom = mixed_in[TOP, :], mixed_in[BOTTOM, :]
    side[TOP, :] = dot(top, columns(weight, place, ACROSS_ABOVE)).astype(BF16)
    side[BOTTOM, :] = dot(bottom, columns(weight, place, ACROSS_BELOW)).astype(BF16)
    for out, which in ((above, ABOVE), (below, BELOW), (across, ACROSS), (own, OWN)):
        out[TOP, :] = dot(top, columns(weight, place, which)).astype(BF16)
        out[BOTTOM, :] = dot(bottom, columns(weight, place, which)).astype(BF16)


def second_kernel(up, down, over, side, above, below, after, top_out, bottom_out, above_out, below_out):
    top_out[...] = (wide(side[TOP, :]) + wide(up[TOP, :])).astype(BF16)
    bottom_out[...] = (wide(side[BOTTOM, :]) + wide(down[TOP, :])).astype(BF16)
    above_out[TOP, :] = (wide(above[TOP, :]) + wide(up[BOTTOM, :])).astype(BF16)
    above_out[BOTTOM, :] = (wide(above[BOTTOM, :]) + wide(over[TOP, :])).astype(BF16)
    below_out[TOP, :] = (wide(below[TOP, :]) + wide(over[BOTTOM, :])).astype(BF16)
    below_out[BOTTOM, :] = (wide(below[BOTTOM, :]) + wide(down[BOTTOM, :])).astype(BF16)


def third_kernel(across, got_t, got_b, after, out):
    out[TOP, :] = (wide(across[TOP, :]) + wide(got_t[...])).astype(BF16)
    out[BOTTOM, :] = (wide(across[BOTTOM, :]) + wide(got_b[...])).astype(BF16)


def last_kernel(own, above, below, across, out):
    inner = wide(own[...]) + wide(above[...])
    out[...] = (inner + (wide(below[...]) + wide(across[...]))).astype(BF16)


def grad_kernel(
    place, weight, own, across, below, above, up, down, over, far_t, far_b, query,
    summed, keep, keep_piece, after,
    grad_query, grad_conv, starts, total,
    full, signal, ends,
):
    halves = (
        (TOP, ((up, TOP, ACROSS_BELOW), (over, BOTTOM, ACROSS_ABOVE), (up, BOTTOM, FAR), (far_t, TOP, ACROSS_FAR))),
        (BOTTOM, ((over, TOP, ACROSS_BELOW), (down, TOP, ACROSS_ABOVE), (down, BOTTOM, FAR), (far_b, TOP, ACROSS_FAR))),
    )
    for rows, parts in halves:
        grad = turned(own[rows, :], columns(weight, place, OWN))
        for ref, which in ((across, ACROSS), (below, BELOW), (above, ABOVE)):
            grad += turned(ref[rows, :], columns(weight, place, which))
        for ref, part, which in parts:
            grad += turned(ref[part, :], columns(weight, place, which))
        full[rows, :] = grad
    for tile in PER_TILE:
        at = tile_of(tile)
        grad_query[:, at] = (full[:, at] * summed[:, at]).astype(BF16)
        conv = (full[:, at] * wide(query[:, at])).astype(BF16)
        grad_conv[:, at] = conv
        signal[tile] = wide(conv)
        ends_of(signal, ends, keep, tile, True)
        chain(ends, starts, total, keep_piece, tile, True)


def back_kernel(
    spot, rates, two, three_off, six_off, before,
    grad_conv, starts, keep, keep_piece, gain, skip, key, value,
    grad_key, grad_value,
    signal, result, begin,
):
    for tile in PER_TILE:
        at = tile_of(tile)
        signal[tile] = wide(grad_conv[:, at])
        core, high, z = spot_of(spot, True)
        over = over_of(rates[tile], z, two[tile], three_off[tile], six_off[tile])
        initial = power(rates[tile], 2 * high + core) * over + before[tile]
        whole_starts(starts, initial, begin, keep_piece, tile, True)
        responses(signal, begin, result, keep, gain, tile, True)
        back = wide(result[tile].astype(BF16))
        total = back + skip[0:1, at] * signal[tile]
        grad_key[:, at] = (total * wide(value[:, at])).astype(BF16)
        grad_value[:, at] = (total * wide(key[:, at])).astype(BF16)


STATE_SHAPE, BLOCK, HALVED = (TILES, MODES, LANES), (ROWS, COLS), (HALF, COLS)
TABLE, DEEP = (TILES, PARTS * MODES, LANES), (TILES, ROWS, LANES)


def call(kernel, outs, scratch, micros, mib, *args):
    return pl.pallas_call(
        kernel,
        out_shape=[jax.ShapeDtypeStruct(shape, kind) for shape, kind in outs],
        in_specs=[SMEM if arg.dtype == jnp.int32 else VMEM for arg in args],
        out_specs=[VMEM] * len(outs),
        scratch_shapes=[pltpu.VMEM(shape, kind) for shape, kind in scratch],
        cost_estimate=pl.CostEstimate(
            flops=int(micros * 1.1e9), bytes_accessed=int(micros * 3e6), transcendentals=0
        ),
        compiler_params=pltpu.CompilerParams(vmem_limit_bytes=mib * 1024 * 1024),
    )(*args)


def tp_perm(move):
    return [(x * 4 + y, move(x, y)[0] % 2 * 4 + move(x, y)[1] % 4) for x in range(2) for y in range(4)]


def ctx_perm(move):
    pairs = []
    for z in range(8):
        for h in range(2):
            for c in range(2):
                to = move(z, h, c)
                pairs.append((z * 4 + h * 2 + c, to[0] % 8 * 4 + to[1] % 2 * 2 + to[2] % 2))
    return pairs


def shift_x(value):
    return lax.ppermute(value, "tp", tp_perm(lambda x, y: (x + 1, y)))


def shift_up(value):
    return lax.ppermute(value, "tp", tp_perm(lambda x, y: (x, y + 1)))


def shift_down(value):
    return lax.ppermute(value, "tp", tp_perm(lambda x, y: (x, y + 3)))


def small(kernel, flipped, *args):
    both = [(STATE_SHAPE, F32)] * 2
    return call(functools.partial(kernel, flipped), both, [], 1.0, 4, *args)


def other_core(value):
    return lax.ppermute(value, "ctx", ctx_perm(lambda z, h, c: (z, h, c + 1)))


def other_half(value):
    return lax.ppermute(value, "ctx", ctx_perm(lambda z, h, c: (z, h + 1, c)))


def earlier(value, k, flipped):
    move = -k if flipped else k
    return lax.ppermute(value, "ctx", ctx_perm(lambda z, h, c: (z + move, h, c)))


def per_device(query, key, value, cotangent, weight, decay_rates, residues, skip_gain):
    at, line = lax.axis_index("tp"), lax.axis_index("ctx")
    x, y = at // 4, at % 4
    place = jnp.stack([(x + dx) % 2 * 4 + (y + dy + 4) % 4 for dx, dy in NEAR]).astype(jnp.int32)
    spot = jnp.stack([line % 2, line // 2 % 2, line // 4]).astype(jnp.int32)
    decay_rates, residues = decay_rates.T, residues.T
    amplitude = residues * jnp.sqrt(-jnp.expm1(-2.0 * decay_rates))
    skip = skip_gain.reshape(1, COLS)

    across = shift_x(cotangent)
    below = shift_up(cotangent)
    above = shift_down(cotangent)
    deep, table, state = (DEEP, F32), (TABLE, F32), (STATE_SHAPE, F32)
    gated = (key.astype(F32) * value.astype(F32)).astype(BF16)
    rates, keep, keep_piece, gain, starts, total = call(
        gate_kernel, [state] * 4 + [table, state], [deep, table], 2.4, 6, spot, place, gated, decay_rates, amplitude
    )
    pair, before = small(pair_kernel, False, spot, rates, total, other_core(total))
    s_up, s_down, s_over = call(
        pack_kernel, [(BLOCK, BF16)] * 3, [], 0.1, 4, across, below, above, pair
    )
    up, down, over = shift_up(s_up), shift_down(s_down), shift_x(s_over)
    packed = s_up
    s_far_t, s_far_b = call(halve_kernel, [(HALVED, BF16)] * 2, [], 0.1, 4, up, down, over)
    far_t, far_b = shift_up(s_far_t), shift_down(s_far_b)

    offs = earlier(pair, 1, False), earlier(pair, 2, False)
    two, three = small(three_kernel, False, spot, rates, pair, *offs)
    offs = earlier(three, 3, False), earlier(three, 6, False)
    over_state, sent = small(sent_kernel, False, spot, rates, pair, two, *offs, packed)
    carried = other_half(sent), over_state, before
    summed, mixed_in = call(
        mix_kernel,
        [(BLOCK, F32), (BLOCK, BF16)],
        [deep, deep, table],
        4.5,
        8,
        spot,
        rates,
        *carried,
        gated,
        starts,
        keep,
        keep_piece,
        gain,
        skip,
        query,
        s_far_t,
        s_far_b,
    )
    s_up, s_down, s_over = call(
        first_kernel, [(BLOCK, BF16)] * 3, [], 1.5, 6, place, mixed_in, weight, far_t, far_b
    )
    g_up, g_down, g_over = shift_up(s_up), shift_down(s_down), shift_x(s_over)
    grad_query, grad_conv, back_starts, back_total = call(
        grad_kernel,
        [(BLOCK, BF16), (BLOCK, BF16), table, state],
        [(BLOCK, F32), deep, table],
        6.0,
        8,
        place,
        weight,
        cotangent,
        across,
        below,
        above,
        up,
        down,
        over,
        far_t,
        far_b,
        query,
        summed,
        keep,
        keep_piece,
        s_up,
    )
    pair, before = small(pair_kernel, True, spot, rates, back_total, other_core(back_total))
    half_other = other_half(pair)
    side, above_part, below_part, across_part, own_part = call(
        rest_kernel, [(BLOCK, BF16)] * 5, [], 2.0, 6, place, mixed_in, weight, pair
    )
    group, before = small(group_kernel, True, spot, rates, pair, before, half_other)
    offs = earlier(group, 1, True), earlier(group, 2, True)
    two, three = small(three_kernel, True, spot, rates, group, *offs)
    offs = earlier(three, 3, True), earlier(three, 6, True)

    s_t, s_b, s_above, s_below = call(
        second_kernel,
        [(HALVED, BF16)] * 2 + [(BLOCK, BF16)] * 2,
        [],
        0.1,
        4,
        g_up,
        g_down,
        g_over,
        side,
        above_part,
        below_part,
        group,
    )
    g_t, g_b = shift_up(s_t), shift_down(s_b)
    g_above, g_below = shift_up(s_above), shift_down(s_below)
    (s_across,) = call(third_kernel, [(BLOCK, BF16)], [], 0.5, 4, across_part, g_t, g_b, three)
    (mixed,) = call(
        last_kernel, [(BLOCK, BF16)], [], 0.1, 4, own_part, g_above, g_below, shift_x(s_across)
    )
    grad_key, grad_value = call(
        back_kernel,
        [(BLOCK, BF16)] * 2,
        [deep, deep, table],
        4.5,
        8,
        spot,
        rates,
        two,
        *offs,
        before,
        grad_conv,
        back_starts,
        keep,
        keep_piece,
        gain,
        skip,
        key,
        value,
    )
    return mixed, grad_query, grad_key, grad_value


def solution(mesh):
    split, rows = P("ctx", "tp"), P("tp", None)
    return jax.shard_map(
        per_device,
        mesh=mesh,
        in_specs=(split, split, split, split, rows, rows, rows, P("tp")),
        out_specs=(split, split, split, split),
        check_vma=False,
    )
```

```python
import functools

import jax
import jax.numpy as jnp
from jax import lax
from jax.experimental import pallas as pl
from jax.experimental.pallas import tpu as pltpu
from jax.sharding import PartitionSpec as P

F32, BF16 = jnp.float32, jnp.bfloat16
ROWS, COLS, MODES, LANES = 512, 512, 16, 128
HALF = ROWS // 2
TILES = COLS // LANES
PARTS = 8
STEP = ROWS // PARTS
APART = STEP + 8
VMEM = pl.BlockSpec(memory_space=pltpu.VMEM)
SMEM = pl.BlockSpec(memory_space=pltpu.SMEM)


def tile_of(tile):
    return slice(tile * LANES, (tile + 1) * LANES)


def spread(ref, tile, mode):
    return jnp.broadcast_to(ref[tile, mode : mode + 1, :], (PARTS, LANES))


def lay(table, tile, values):
    for piece in range(PARTS):
        rows = slice(piece * APART, piece * APART + STEP)
        table[tile, rows, :] = values[piece * STEP : (piece + 1) * STEP, :]


def laid(table, tile):
    starts = range(0, PARTS * APART, APART)
    return jnp.concatenate([table[tile, start : start + STEP, :] for start in starts])


def ends_of(signal, ends, keep, tile, flipped):
    decay = [spread(keep, tile, m) for m in range(MODES)]

    def step(i, states):
        at = STEP - 1 - i if flipped else i
        u = signal[tile, pl.ds(at, PARTS, stride=APART), :]
        return tuple(decay[m] * states[m] + u for m in range(MODES))

    zero = jnp.zeros((PARTS, LANES), F32)
    states = lax.fori_loop(0, STEP, step, (zero,) * MODES, unroll=16)
    for m in range(MODES):
        ends[tile, pl.ds(m, PARTS, stride=MODES), :] = states[m]


def chain(ends, starts, total, keep_piece, tile, flipped):
    state = jnp.zeros((MODES, LANES), F32)
    factor = keep_piece[tile]
    order = range(PARTS - 1, -1, -1) if flipped else range(PARTS)
    for piece in order:
        rows = slice(piece * MODES, (piece + 1) * MODES)
        starts[tile, rows, :] = state
        state = factor * state + ends[tile, rows, :]
    total[tile] = state


def whole_starts(starts, initial, begin, keep_piece, tile, flipped):
    carried = initial
    factor = keep_piece[tile]
    order = range(PARTS - 1, -1, -1) if flipped else range(PARTS)
    for piece in order:
        rows = slice(piece * MODES, (piece + 1) * MODES)
        begin[tile, rows, :] = starts[tile, rows, :] + carried
        carried = factor * carried


def responses(signal, begin, result, keep, gain, tile, flipped):
    decay = [spread(keep, tile, m) for m in range(MODES)]
    gains = [spread(gain, tile, m) for m in range(MODES)]

    def step(i, states):
        at = STEP - 1 - i if flipped else i
        u = signal[tile, pl.ds(at, PARTS, stride=APART), :]
        states = tuple(decay[m] * states[m] + u for m in range(MODES))
        terms = [gains[m] * states[m] for m in range(MODES)]
        while len(terms) > 1:
            terms = [terms[i] + terms[i + 1] for i in range(0, len(terms), 2)]
        result[tile, pl.ds(at, PARTS, stride=APART), :] = terms[0]
        return states

    states = tuple(begin[tile, pl.ds(m, PARTS, stride=MODES), :] for m in range(MODES))
    lax.fori_loop(0, STEP, step, states, unroll=16)


def dot(a, b):
    return jnp.dot(a, b, preferred_element_type=F32)


def turned(a, b):
    return lax.dot_general(a, b, (((1,), (1,)), ((), ())), preferred_element_type=F32)


def wide(value):
    return value.astype(F32)


def columns(weight, place, which):
    return weight[:, pl.ds(pl.multiple_of(place[which] * COLS, COLS), COLS)]


NEAR = [(0, 0), (1, 0), (0, -1), (0, 1), (1, -1), (1, 1), (0, 2), (1, 2)]
OWN, ACROSS, BEHIND, AHEAD, ACROSS_BEHIND, ACROSS_AHEAD, FAR, ACROSS_FAR = range(8)
TOP, BOTTOM = slice(0, HALF), slice(HALF, ROWS)
FIRST, SECOND = slice(0, ROWS), slice(ROWS, 2 * ROWS)
PER_TILE = range(TILES)


def gate_kernel(
    spot, place, gated, decay_rates, amplitude, rates, keep, keep_piece, gain, starts, total, signal, ends,
):
    for tile in PER_TILE:
        at = tile_of(tile)
        rates[tile] = decay_rates[:, at]
        gain[tile] = amplitude[:, at]
        keep[tile] = jnp.exp(-rates[tile])
        keep_piece[tile] = jnp.exp(rates[tile] * -float(STEP))
        lay(signal, tile, wide(gated[:, at]))
        ends_of(signal, ends, keep, tile, False)
        chain(ends, starts, total, keep_piece, tile, False)


def power(rates, n):
    return jnp.exp(rates * (-float(ROWS) * jnp.asarray(n).astype(F32)))


def spot_of(spot, flipped):
    core, high, z = spot[0], spot[1], spot[2]
    return (1 - core, 1 - high, 7 - z) if flipped else (core, high, z)


def pair_kernel(flipped, spot, rates, own, other, pair, before):
    core, _, _ = spot_of(spot, flipped)
    pair[...] = power(rates[...], 1 - core) * own[...] + power(rates[...], core) * other[...]
    before[...] = core.astype(F32) * other[...]


def three_kernel(flipped, spot, rates, pair, one_off, two_off, two, three):
    _, _, z = spot_of(spot, flipped)
    here = (z >= 1).astype(F32) * one_off[...]
    here += (z >= 2).astype(F32) * (power(rates[...], 4) * two_off[...])
    two[...] = here
    three[...] = pair[...] + power(rates[...], 4) * here


def over_of(rates, z, two, three_off, six_off):
    here = two + (z >= 3).astype(F32) * (power(rates, 8) * three_off)
    return here + (z >= 6).astype(F32) * (power(rates, 20) * six_off)


def sent_kernel(flipped, spot, rates, pair, two, three_off, six_off, after, over, sent):
    _, high, z = spot_of(spot, flipped)
    here = over_of(rates[...], z, two[...], three_off[...], six_off[...])
    over[...] = here
    later = high.astype(F32)
    sent[...] = later * here + (1.0 - later) * (pair[...] + power(rates[...], 4) * here)


def group_kernel(flipped, spot, rates, pair, before, other, group, before_all):
    core, high, _ = spot_of(spot, flipped)
    early, late = power(rates[...], 2 - 2 * high), power(rates[...], 2 * high)
    group[...] = early * pair[...] + late * other[...]
    before_all[...] = before[...] + high.astype(F32) * (power(rates[...], core) * other[...])


def pack_kernel(across, behind, ahead, after, out):
    out[FIRST, :] = across[...]
    out[SECOND, :] = behind[...]


def halve_kernel(got, after, out):
    out[...] = got[FIRST, :]


def mix_kernel(
    spot, rates, other, over, before,
    gated, starts, keep, keep_piece, gain, skip, query, after,
    summed, mixed_in,
    signal, result, begin,
):
    for tile in PER_TILE:
        at = tile_of(tile)
        lay(signal, tile, wide(gated[:, at]))
        core, _, _ = spot_of(spot, False)
        initial = other[tile] + power(rates[tile], 2) * over[tile]
        initial = power(rates[tile], core) * initial + before[tile]
        whole_starts(starts, initial, begin, keep_piece, tile, False)
        responses(signal, begin, result, keep, gain, tile, False)
        conv = wide(laid(result, tile).astype(BF16))
        total = conv + skip[0:1, at] * wide(gated[:, at])
        summed[:, at] = total
        mixed_in[:, at] = (wide(query[:, at]) * total).astype(BF16)


def products(mixed_in, weight, place, outs):
    for out, start, which in outs:
        for rows in (TOP, BOTTOM):
            part = dot(mixed_in[rows, :], columns(weight, place, which))
            out[start + rows.start : start + rows.stop, :] = part.astype(BF16)


def first_kernel(place, mixed_in, weight, after, along, over):
    outs = ((along, 0, ACROSS_FAR), (along, ROWS, FAR), (over, 0, ACROSS_BEHIND))
    products(mixed_in, weight, place, outs)


def rest_kernel(place, mixed_in, weight, after, side, ahead, behind, across, own):
    outs = ((side, 0, ACROSS_AHEAD), (ahead, 0, AHEAD), (behind, 0, BEHIND))
    products(mixed_in, weight, place, outs + ((across, 0, ACROSS), (own, 0, OWN)))


def second_kernel(along, over, side, ahead, behind, after, side_out, ahead_out, behind_out):
    side_out[...] = (wide(side[...]) + wide(along[FIRST, :])).astype(BF16)
    ahead_out[...] = (wide(ahead[...]) + wide(along[SECOND, :])).astype(BF16)
    behind_out[...] = (wide(behind[...]) + wide(over[...])).astype(BF16)


def third_kernel(across, got, after, out):
    out[...] = (wide(across[...]) + wide(got[...])).astype(BF16)


def last_kernel(own, ahead, behind, across, out):
    inner = wide(own[...]) + wide(ahead[...])
    out[...] = (inner + (wide(behind[...]) + wide(across[...]))).astype(BF16)


def early_kernel(place, weight, own, across, behind, ahead, after, acc):
    blocks = ((own, OWN), (across, ACROSS), (behind, BEHIND), (ahead, AHEAD))
    for rows in (TOP, BOTTOM):
        grad = jnp.zeros((HALF, COLS), F32)
        for ref, which in blocks:
            grad += turned(ref[rows, :], columns(weight, place, which))
        acc[rows, :] = grad


def grad_kernel(
    place, weight, acc, got, over, far, query, summed, keep, keep_piece, after,
    grad_query, grad_conv, starts, total,
    full, signal, ends,
):
    parts = ((got, 0, ACROSS_BEHIND), (got, ROWS, FAR), (over, 0, ACROSS_AHEAD), (far, 0, ACROSS_FAR))
    for rows in (TOP, BOTTOM):
        grad = acc[rows, :]
        for ref, start, which in parts:
            block = ref[start + rows.start : start + rows.stop, :]
            grad += turned(block, columns(weight, place, which))
        full[rows, :] = grad
    for tile in PER_TILE:
        at = tile_of(tile)
        grad_query[:, at] = (full[:, at] * summed[:, at]).astype(BF16)
        conv = (full[:, at] * wide(query[:, at])).astype(BF16)
        grad_conv[:, at] = conv
        lay(signal, tile, wide(conv))
        ends_of(signal, ends, keep, tile, True)
        chain(ends, starts, total, keep_piece, tile, True)


def back_kernel(
    spot, rates, two, three_off, six_off, before,
    grad_conv, starts, keep, keep_piece, gain, skip, key, value,
    grad_key, grad_value,
    signal, result, begin,
):
    for tile in PER_TILE:
        at = tile_of(tile)
        lay(signal, tile, wide(grad_conv[:, at]))
        core, high, z = spot_of(spot, True)
        over = over_of(rates[tile], z, two[tile], three_off[tile], six_off[tile])
        initial = power(rates[tile], 2 * high + core) * over + before[tile]
        whole_starts(starts, initial, begin, keep_piece, tile, True)
        responses(signal, begin, result, keep, gain, tile, True)
        back = wide(laid(result, tile).astype(BF16))
        total = back + skip[0:1, at] * wide(grad_conv[:, at])
        grad_key[:, at] = (total * wide(value[:, at])).astype(BF16)
        grad_value[:, at] = (total * wide(key[:, at])).astype(BF16)


STATE_SHAPE, BLOCK, TWICE = (TILES, MODES, LANES), (ROWS, COLS), (2 * ROWS, COLS)
TABLE, DEEP = (TILES, PARTS * MODES, LANES), (TILES, PARTS * APART, LANES)


def call(kernel, outs, scratch, micros, mib, *args):
    return pl.pallas_call(
        kernel,
        out_shape=[jax.ShapeDtypeStruct(shape, kind) for shape, kind in outs],
        in_specs=[SMEM if arg.dtype == jnp.int32 else VMEM for arg in args],
        out_specs=[VMEM] * len(outs),
        scratch_shapes=[pltpu.VMEM(shape, kind) for shape, kind in scratch],
        cost_estimate=pl.CostEstimate(
            flops=int(micros * 1.1e9), bytes_accessed=int(micros * 3e6), transcendentals=0
        ),
        compiler_params=pltpu.CompilerParams(vmem_limit_bytes=mib * 1024 * 1024),
    )(*args)


def ctx_perm(move):
    pairs = []
    for z in range(8):
        for h in range(2):
            for c in range(2):
                to = move(z, h, c)
                pairs.append((z * 4 + h * 2 + c, to[0] % 8 * 4 + to[1] % 2 * 2 + to[2] % 2))
    return pairs


def shift_x(value):
    return lax.ppermute(value, "tp", [(at, (at + 4) % 8) for at in range(8)])


def along_y(value, turn):
    pairs = []
    for line in range(32):
        step = turn * (1 - 2 * (line % 2))
        for at in range(8):
            pairs.append((line * 8 + at, line * 8 + at // 4 * 4 + (at + step) % 4))
    return lax.ppermute(value, ("ctx", "tp"), pairs)


def small(kernel, flipped, *args):
    both = [(STATE_SHAPE, F32)] * 2
    return call(functools.partial(kernel, flipped), both, [], 1.0, 4, *args)


def other_core(value):
    return lax.ppermute(value, "ctx", ctx_perm(lambda z, h, c: (z, h, c + 1)))


def other_half(value):
    return lax.ppermute(value, "ctx", ctx_perm(lambda z, h, c: (z, h + 1, c)))


def earlier(value, k, flipped):
    move = -k if flipped else k
    return lax.ppermute(value, "ctx", ctx_perm(lambda z, h, c: (z + move, h, c)))


def per_device(query, key, value, cotangent, weight, decay_rates, residues, skip_gain):
    at, line = lax.axis_index("tp"), lax.axis_index("ctx")
    x, y = at // 4, at % 4
    step = 1 - 2 * (line % 2)
    place = [(x + dx) % 2 * 4 + (y + step * dy + 4) % 4 for dx, dy in NEAR]
    place = jnp.stack(place).astype(jnp.int32)
    spot = jnp.stack([line % 2, line // 2 % 2, line // 4]).astype(jnp.int32)
    decay_rates, residues = decay_rates.T, residues.T
    amplitude = residues * jnp.sqrt(-jnp.expm1(-2.0 * decay_rates))
    skip = skip_gain.reshape(1, COLS)

    across = shift_x(cotangent)
    behind = along_y(cotangent, 1)
    ahead = along_y(cotangent, -1)

    deep, table, state = (DEEP, F32), (TABLE, F32), (STATE_SHAPE, F32)
    gated = (key.astype(F32) * value.astype(F32)).astype(BF16)
    rates, keep, keep_piece, gain, starts, total = call(
        gate_kernel, [state] * 4 + [table, state], [deep, table], 2.4, 6, spot, place, gated, decay_rates, amplitude
    )
    pair, before = small(pair_kernel, False, spot, rates, total, other_core(total))
    offs = earlier(pair, 1, False), earlier(pair, 2, False)
    (packed,) = call(pack_kernel, [(TWICE, BF16)], [], 1.0, 4, across, behind, ahead, offs[0])
    got, over = along_y(packed, 1), shift_x(ahead)
    (s_far,) = call(halve_kernel, [(BLOCK, BF16)], [], 1.0, 4, got, over)
    far = along_y(s_far, 1)
    (acc,) = call(
        early_kernel,
        [(BLOCK, F32)],
        [],
        2.0,
        6,
        place,
        weight,
        cotangent,
        across,
        behind,
        ahead,
        packed,
    )

    two, three = small(three_kernel, False, spot, rates, pair, *offs)
    offs = earlier(three, 3, False), earlier(three, 6, False)
    over_state, sent = small(sent_kernel, False, spot, rates, pair, two, *offs, acc)
    carried = other_half(sent), over_state, before
    summed, mixed_in = call(
        mix_kernel,
        [(BLOCK, F32), (BLOCK, BF16)],
        [deep, deep, table],
        4.5,
        8,
        spot,
        rates,
        *carried,
        gated,
        starts,
        keep,
        keep_piece,
        gain,
        skip,
        query,
        s_far,
    )
    s_along, s_over = call(
        first_kernel,
        [(TWICE, BF16), (BLOCK, BF16)],
        [],
        1.5,
        6,
        place,
        mixed_in,
        weight,
        far,
    )
    g_along, g_over = along_y(s_along, 1), shift_x(s_over)
    grad_query, grad_conv, back_starts, back_total = call(
        grad_kernel,
        [(BLOCK, BF16), (BLOCK, BF16), table, state],
        [(BLOCK, F32), deep, table],
        6.0,
        8,
        place,
        weight,
        acc,
        got,
        over,
        far,
        query,
        summed,
        keep,
        keep_piece,
        s_along,
    )
    pair, before = small(pair_kernel, True, spot, rates, back_total, other_core(back_total))
    half_other = other_half(pair)
    side, ahead_part, behind_part, across_part, own_part = call(
        rest_kernel, [(BLOCK, BF16)] * 5, [], 2.0, 6, place, mixed_in, weight, pair
    )
    group, before = small(group_kernel, True, spot, rates, pair, before, half_other)
    offs = earlier(group, 1, True), earlier(group, 2, True)
    two, three = small(three_kernel, True, spot, rates, group, *offs)
    offs = earlier(three, 3, True), earlier(three, 6, True)

    s_side, s_ahead, s_behind = call(
        second_kernel,
        [(BLOCK, BF16)] * 3,
        [],
        3.0,
        4,
        g_along,
        g_over,
        side,
        ahead_part,
        behind_part,
        group,
    )
    g_side, g_ahead, g_behind = along_y(s_side, 1), along_y(s_ahead, 1), along_y(s_behind, -1)
    (s_across,) = call(third_kernel, [(BLOCK, BF16)], [], 0.5, 4, across_part, g_side, three)
    (mixed,) = call(
        last_kernel, [(BLOCK, BF16)], [], 0.5, 4, own_part, g_ahead, g_behind, shift_x(s_across)
    )
    grad_key, grad_value = call(
        back_kernel,
        [(BLOCK, BF16)] * 2,
        [deep, deep, table],
        4.5,
        8,
        spot,
        rates,
        two,
        *offs,
        before,
        grad_conv,
        back_starts,
        keep,
        keep_piece,
        gain,
        skip,
        key,
        value,
    )
    return mixed, grad_query, grad_key, grad_value


def solution(mesh):
    split, rows = P("ctx", "tp"), P("tp", None)
    return jax.shard_map(
        per_device,
        mesh=mesh,
        in_specs=(split, split, split, split, rows, rows, rows, P("tp")),
        out_specs=(split, split, split, split),
        check_vma=False,
    )
```

```python
import functools

import jax
import jax.numpy as jnp
from jax import lax
from jax.experimental import pallas as pl
from jax.experimental.pallas import tpu as pltpu
from jax.sharding import PartitionSpec as P

F32, BF16 = jnp.float32, jnp.bfloat16
ROWS, COLS, MODES, LANES = 512, 512, 16, 128
HALF = ROWS // 2
TILES = COLS // LANES
PARTS = 8
STEP = ROWS // PARTS
APART = STEP + 8
VMEM = pl.BlockSpec(memory_space=pltpu.VMEM)


def tile_of(tile):
    return slice(tile * LANES, (tile + 1) * LANES)


def spread(ref, tile, mode):
    return jnp.broadcast_to(ref[tile, mode : mode + 1, :], (PARTS, LANES))


def lay(table, tile, values):
    for piece in range(PARTS):
        rows = slice(piece * APART, piece * APART + STEP)
        table[tile, rows, :] = values[piece * STEP : (piece + 1) * STEP, :]


def laid(table, tile):
    starts = range(0, PARTS * APART, APART)
    return jnp.concatenate([table[tile, start : start + STEP, :] for start in starts])


def ends_of(signal, ends, keep, tile, flipped):
    decay = [spread(keep, tile, m) for m in range(MODES)]

    def step(i, states):
        at = STEP - 1 - i if flipped else i
        u = signal[tile, pl.ds(at, PARTS, stride=APART), :]
        return tuple(decay[m] * states[m] + u for m in range(MODES))

    zero = jnp.zeros((PARTS, LANES), F32)
    states = lax.fori_loop(0, STEP, step, (zero,) * MODES, unroll=16)
    for m in range(MODES):
        ends[tile, pl.ds(m, PARTS, stride=MODES), :] = states[m]


def chain(ends, starts, total, keep_piece, tile, flipped):
    state = jnp.zeros((MODES, LANES), F32)
    factor = keep_piece[tile]
    order = range(PARTS - 1, -1, -1) if flipped else range(PARTS)
    for piece in order:
        rows = slice(piece * MODES, (piece + 1) * MODES)
        starts[tile, rows, :] = state
        state = factor * state + ends[tile, rows, :]
    total[tile] = state


def whole_starts(starts, initial, begin, keep_piece, tile, flipped):
    carried = initial
    factor = keep_piece[tile]
    order = range(PARTS - 1, -1, -1) if flipped else range(PARTS)
    for piece in order:
        rows = slice(piece * MODES, (piece + 1) * MODES)
        begin[tile, rows, :] = starts[tile, rows, :] + carried
        carried = factor * carried


def responses(signal, begin, result, keep, gain, tile, flipped):
    decay = [spread(keep, tile, m) for m in range(MODES)]
    gains = [spread(gain, tile, m) for m in range(MODES)]

    def step(i, states):
        at = STEP - 1 - i if flipped else i
        u = signal[tile, pl.ds(at, PARTS, stride=APART), :]
        states = tuple(decay[m] * states[m] + u for m in range(MODES))
        terms = [gains[m] * states[m] for m in range(MODES)]
        while len(terms) > 1:
            terms = [terms[i] + terms[i + 1] for i in range(0, len(terms), 2)]
        result[tile, pl.ds(at, PARTS, stride=APART), :] = terms[0]
        return states

    states = tuple(begin[tile, pl.ds(m, PARTS, stride=MODES), :] for m in range(MODES))
    lax.fori_loop(0, STEP, step, states, unroll=16)


def dot(a, b):
    return jnp.dot(a, b, preferred_element_type=F32)


def turned(a, b):
    return lax.dot_general(a, b, (((1,), (1,)), ((), ())), preferred_element_type=F32)


def wide(value):
    return value.astype(F32)


NEAR = [(0, 0), (1, 0), (0, -1), (0, 1), (1, -1), (1, 1), (0, 2), (1, 2)]
OWN, ACROSS, BEHIND, AHEAD, ACROSS_BEHIND, ACROSS_AHEAD, FAR, ACROSS_FAR = range(8)
TOP, BOTTOM = slice(0, HALF), slice(HALF, ROWS)
FIRST, SECOND = slice(0, ROWS), slice(ROWS, 2 * ROWS)
PER_TILE = range(TILES)


def columns(weight, which):
    at, step = lax.axis_index("tp"), 1 - 2 * lax.rem(lax.axis_index("ctx"), 2)
    dx, dy = NEAR[which]
    x = lax.rem(lax.div(at, 4) + dx, 2)
    y = lax.rem(lax.rem(at, 4) + step * dy + 4, 4)
    return weight[:, pl.ds(pl.multiple_of((x * 4 + y) * COLS, COLS), COLS)]


def gate_kernel(
    gated, fading, amplitude, rates, keep, keep_piece, gain, starts, total, signal, ends,
):
    for tile in PER_TILE:
        at = tile_of(tile)
        rates[tile] = -fading[:, at]
        gain[tile] = amplitude[:, at]
        keep[tile] = jnp.exp(-rates[tile])
        keep_piece[tile] = jnp.exp(rates[tile] * -float(STEP))
        lay(signal, tile, wide(gated[:, at]))
        ends_of(signal, ends, keep, tile, False)
        chain(ends, starts, total, keep_piece, tile, False)


def power(rates, n):
    return jnp.exp(rates * (-float(ROWS) * jnp.asarray(n).astype(F32)))


def spot_of(flipped):
    line = lax.axis_index("ctx")
    core, high, z = lax.rem(line, 2), lax.rem(lax.div(line, 2), 2), lax.div(line, 4)
    return (1 - core, 1 - high, 7 - z) if flipped else (core, high, z)


def pair_kernel(flipped, rates, own, other, pair, before):
    core, _, _ = spot_of(flipped)
    pair[...] = power(rates[...], 1 - core) * own[...] + power(rates[...], core) * other[...]
    before[...] = core.astype(F32) * other[...]


def three_kernel(flipped, rates, pair, one_off, two_off, two, three):
    _, _, z = spot_of(flipped)
    here = (z >= 1).astype(F32) * one_off[...]
    here += (z >= 2).astype(F32) * (power(rates[...], 4) * two_off[...])
    two[...] = here
    three[...] = pair[...] + power(rates[...], 4) * here


def over_of(rates, z, two, three_off, six_off):
    here = two + (z >= 3).astype(F32) * (power(rates, 8) * three_off)
    return here + (z >= 6).astype(F32) * (power(rates, 20) * six_off)


def sent_kernel(flipped, rates, pair, two, three_off, six_off, after, after_too, over, sent):
    _, high, z = spot_of(flipped)
    here = over_of(rates[...], z, two[...], three_off[...], six_off[...])
    over[...] = here
    later = high.astype(F32)
    sent[...] = later * here + (1.0 - later) * (pair[...] + power(rates[...], 4) * here)


def group_kernel(flipped, rates, pair, before, other, group, before_all):
    core, high, _ = spot_of(flipped)
    early, late = power(rates[...], 2 - 2 * high), power(rates[...], 2 * high)
    group[...] = early * pair[...] + late * other[...]
    before_all[...] = before[...] + high.astype(F32) * (power(rates[...], core) * other[...])


def relay_kernel(across, behind, ahead, after, after_too, across_out, behind_out):
    across_out[...] = across[...]
    behind_out[...] = behind[...]


def mix_kernel(
    rates, other, over, before,
    gated, starts, keep, keep_piece, gain, skip, query, after,
    summed, mixed_in,
    signal, result, begin,
):
    for tile in PER_TILE:
        at = tile_of(tile)
        lay(signal, tile, wide(gated[:, at]))
        core, _, _ = spot_of(False)
        initial = other[tile] + power(rates[tile], 2) * over[tile]
        initial = power(rates[tile], core) * initial + before[tile]
        whole_starts(starts, initial, begin, keep_piece, tile, False)
        responses(signal, begin, result, keep, gain, tile, False)
        conv = wide(laid(result, tile).astype(BF16))
        total = conv + skip[0:1, at] * wide(gated[:, at])
        summed[:, at] = total
        mixed_in[:, at] = (wide(query[:, at]) * total).astype(BF16)


def products(mixed_in, weight, outs):
    for out, start, which in outs:
        for rows in (TOP, BOTTOM):
            part = dot(mixed_in[rows, :], columns(weight, which))
            out[start + rows.start : start + rows.stop, :] = part.astype(BF16)


def first_kernel(mixed_in, weight, across_far, far):
    products(mixed_in, weight, ((across_far, 0, ACROSS_FAR), (far, 0, FAR)))


def rest_kernel(mixed_in, weight, after, over, side, ahead, behind, across, own):
    outs = ((over, 0, ACROSS_BEHIND), (side, 0, ACROSS_AHEAD), (ahead, 0, AHEAD))
    products(mixed_in, weight, outs + ((behind, 0, BEHIND), (across, 0, ACROSS), (own, 0, OWN)))


def side_kernel(got, side, after, out):
    out[...] = (wide(side[...]) + wide(got[...])).astype(BF16)


def second_kernel(along, over, ahead, behind, after, ahead_out, behind_out):
    ahead_out[...] = (wide(ahead[...]) + wide(along[...])).astype(BF16)
    behind_out[...] = (wide(behind[...]) + wide(over[...])).astype(BF16)


def third_kernel(across, got, after, out):
    out[...] = (wide(across[...]) + wide(got[...])).astype(BF16)


def last_kernel(own, ahead, behind, across, out):
    inner = wide(own[...]) + wide(ahead[...])
    out[...] = (inner + (wide(behind[...]) + wide(across[...]))).astype(BF16)


def early_kernel(weight, own, across, behind, ahead, after, acc):
    blocks = ((own, OWN), (across, ACROSS), (behind, BEHIND), (ahead, AHEAD))
    for rows in (TOP, BOTTOM):
        grad = jnp.zeros((HALF, COLS), F32)
        for ref, which in blocks:
            grad += turned(ref[rows, :], columns(weight, which))
        acc[rows, :] = grad


def later_kernel(weight, acc, got_across, got_behind, over, total):
    parts = ((got_across, ACROSS_BEHIND), (got_behind, FAR), (over, ACROSS_AHEAD))
    for rows in (TOP, BOTTOM):
        grad = acc[rows, :]
        for ref, which in parts:
            grad += turned(ref[rows, :], columns(weight, which))
        total[rows, :] = grad


def grad_kernel(
    weight, acc, far, query, summed, keep, keep_piece, after,
    grad_query, grad_conv, starts, total,
    full, signal, ends,
):
    for rows in (TOP, BOTTOM):
        grad = acc[rows, :] + turned(far[rows, :], columns(weight, ACROSS_FAR))
        full[rows, :] = grad
    for tile in PER_TILE:
        at = tile_of(tile)
        grad_query[:, at] = (full[:, at] * summed[:, at]).astype(BF16)
        conv = (full[:, at] * wide(query[:, at])).astype(BF16)
        grad_conv[:, at] = conv
        lay(signal, tile, wide(conv))
        ends_of(signal, ends, keep, tile, True)
        chain(ends, starts, total, keep_piece, tile, True)


def back_kernel(
    rates, two, three_off, six_off, before,
    grad_conv, starts, keep, keep_piece, gain, skip, key, value,
    grad_key, grad_value,
    signal, result, begin,
):
    for tile in PER_TILE:
        at = tile_of(tile)
        lay(signal, tile, wide(grad_conv[:, at]))
        core, high, z = spot_of(True)
        over = over_of(rates[tile], z, two[tile], three_off[tile], six_off[tile])
        initial = power(rates[tile], 2 * high + core) * over + before[tile]
        whole_starts(starts, initial, begin, keep_piece, tile, True)
        responses(signal, begin, result, keep, gain, tile, True)
        back = wide(laid(result, tile).astype(BF16))
        total = back + skip[0:1, at] * wide(grad_conv[:, at])
        grad_key[:, at] = (total * wide(value[:, at])).astype(BF16)
        grad_value[:, at] = (total * wide(key[:, at])).astype(BF16)


STATE_SHAPE, BLOCK, TWICE = (TILES, MODES, LANES), (ROWS, COLS), (2 * ROWS, COLS)
TABLE, DEEP = (TILES, PARTS * MODES, LANES), (TILES, PARTS * APART, LANES)


def call(kernel, outs, scratch, micros, mib, *args):
    return pl.pallas_call(
        kernel,
        out_shape=[jax.ShapeDtypeStruct(shape, kind) for shape, kind in outs],
        in_specs=[VMEM] * len(args),
        out_specs=[VMEM] * len(outs),
        scratch_shapes=[pltpu.VMEM(shape, kind) for shape, kind in scratch],
        cost_estimate=pl.CostEstimate(
            flops=int(micros * 1.1e9), bytes_accessed=int(micros * 3e6), transcendentals=0
        ),
        compiler_params=pltpu.CompilerParams(vmem_limit_bytes=mib * 1024 * 1024),
    )(*args)


def ctx_perm(move):
    pairs = []
    for z in range(8):
        for h in range(2):
            for c in range(2):
                to = move(z, h, c)
                pairs.append((z * 4 + h * 2 + c, to[0] % 8 * 4 + to[1] % 2 * 2 + to[2] % 2))
    return pairs


def shift_x(value):
    return lax.ppermute(value, "tp", [(at, (at + 4) % 8) for at in range(8)])


def along_y(value, turn):
    pairs = []
    for line in range(32):
        step = turn * (1 - 2 * (line % 2))
        for at in range(8):
            pairs.append((line * 8 + at, line * 8 + at // 4 * 4 + (at + step) % 4))
    return lax.ppermute(value, ("ctx", "tp"), pairs)


def small(kernel, flipped, *args):
    both = [(STATE_SHAPE, F32)] * 2
    return call(functools.partial(kernel, flipped), both, [], 1.0, 4, *args)


def other_core(value):
    return lax.ppermute(value, "ctx", ctx_perm(lambda z, h, c: (z, h, c + 1)))


def other_half(value):
    return lax.ppermute(value, "ctx", ctx_perm(lambda z, h, c: (z, h + 1, c)))


def earlier(value, k, flipped):
    move = -k if flipped else k
    return lax.ppermute(value, "ctx", ctx_perm(lambda z, h, c: (z + move, h, c)))


def per_device(query, key, value, cotangent, weight, decay_rates, residues, skip_gain):
    decay_rates, residues = decay_rates.T, residues.T
    amplitude = residues * jnp.sqrt(-jnp.expm1(-2.0 * decay_rates))
    fading = -decay_rates
    skip = skip_gain.reshape(1, COLS)

    across = shift_x(cotangent)
    behind = along_y(cotangent, 1)
    ahead = along_y(cotangent, -1)

    deep, table, state = (DEEP, F32), (TABLE, F32), (STATE_SHAPE, F32)
    gated = (key.astype(F32) * value.astype(F32)).astype(BF16)
    rates, keep, keep_piece, gain, starts, total = call(
        gate_kernel, [state] * 4 + [table, state], [deep, table], 2.4, 6, gated, fading, amplitude
    )
    pair, before = small(pair_kernel, False, rates, total, other_core(total))
    offs = earlier(pair, 1, False), earlier(pair, 2, False)
    s_across, s_behind = call(
        relay_kernel, [(BLOCK, BF16)] * 2, [], 1.0, 4, across, behind, ahead, *offs
    )
    got_across, got_behind, over = along_y(s_across, 1), along_y(s_behind, 1), shift_x(ahead)
    far = along_y(got_across, 1)
    (acc,) = call(
        early_kernel,
        [(BLOCK, F32)],
        [],
        2.0,
        6,
        weight,
        cotangent,
        across,
        behind,
        ahead,
        s_across,
    )

    two, three = small(three_kernel, False, rates, pair, *offs)
    offs = earlier(three, 3, False), earlier(three, 6, False)
    over_state, sent = small(sent_kernel, False, rates, pair, two, *offs, acc, got_across)
    (acc,) = call(
        later_kernel, [(BLOCK, F32)], [], 1.5, 6, weight, acc, got_across, got_behind, over
    )
    carried = other_half(sent), over_state, before
    summed, mixed_in = call(
        mix_kernel,
        [(BLOCK, F32), (BLOCK, BF16)],
        [deep, deep, table],
        4.5,
        8,
        rates,
        *carried,
        gated,
        starts,
        keep,
        keep_piece,
        gain,
        skip,
        query,
        got_across,
    )
    s_across_far, s_along = call(
        first_kernel, [(BLOCK, BF16)] * 2, [], 1.0, 6, mixed_in, weight
    )
    g_across_far, g_along = along_y(s_across_far, 1), along_y(s_along, 1)
    grad_query, grad_conv, back_starts, back_total = call(
        grad_kernel,
        [(BLOCK, BF16), (BLOCK, BF16), table, state],
        [(BLOCK, F32), deep, table],
        6.0,
        8,
        weight,
        acc,
        far,
        query,
        summed,
        keep,
        keep_piece,
        s_along,
    )
    pair, before = small(pair_kernel, True, rates, back_total, other_core(back_total))
    half_other = other_half(pair)
    s_over, side, ahead_part, behind_part, across_part, own_part = call(
        rest_kernel, [(BLOCK, BF16)] * 6, [], 2.0, 6, mixed_in, weight, pair
    )
    group, before = small(group_kernel, True, rates, pair, before, half_other)
    offs = earlier(group, 1, True), earlier(group, 2, True)
    two, three = small(three_kernel, True, rates, group, *offs)
    offs = earlier(three, 3, True), earlier(three, 6, True)

    g_over = shift_x(s_over)
    (s_side,) = call(side_kernel, [(BLOCK, BF16)], [], 0.5, 4, g_across_far, side, group)
    s_ahead, s_behind = call(
        second_kernel,
        [(BLOCK, BF16)] * 2,
        [],
        1.0,
        4,
        g_along,
        g_over,
        ahead_part,
        behind_part,
        three,
    )
    g_side, g_ahead, g_behind = along_y(s_side, 1), along_y(s_ahead, 1), along_y(s_behind, -1)
    (s_across,) = call(third_kernel, [(BLOCK, BF16)], [], 0.5, 4, across_part, g_side, three)
    (mixed,) = call(
        last_kernel, [(BLOCK, BF16)], [], 0.5, 4, own_part, g_ahead, g_behind, shift_x(s_across)
    )
    grad_key, grad_value = call(
        back_kernel,
        [(BLOCK, BF16)] * 2,
        [deep, deep, table],
        4.5,
        8,
        rates,
        two,
        *offs,
        before,
        grad_conv,
        back_starts,
        keep,
        keep_piece,
        gain,
        skip,
        key,
        value,
    )
    return mixed, grad_query, grad_key, grad_value


def solution(mesh):
    split, rows = P("ctx", "tp"), P("tp", None)
    return jax.shard_map(
        per_device,
        mesh=mesh,
        in_specs=(split, split, split, split, rows, rows, rows, P("tp")),
        out_specs=(split, split, split, split),
        check_vma=False,
    )
```

```python
import functools

import jax
import jax.numpy as jnp
from jax import lax
from jax.experimental import pallas as pl
from jax.experimental.pallas import tpu as pltpu
from jax.sharding import PartitionSpec as P

F32, BF16 = jnp.float32, jnp.bfloat16
ROWS, COLS, MODES, LANES = 512, 512, 16, 128
HALF = ROWS // 2
TILES = COLS // LANES
PARTS = 8
STEP = ROWS // PARTS
APART = STEP + 8
VMEM = pl.BlockSpec(memory_space=pltpu.VMEM)


def tile_of(tile):
    return slice(tile * LANES, (tile + 1) * LANES)


def spread(ref, tile, mode):
    return jnp.broadcast_to(ref[tile, mode : mode + 1, :], (PARTS, LANES))


def lay(table, tile, values):
    for piece in range(PARTS):
        rows = slice(piece * APART, piece * APART + STEP)
        table[tile, rows, :] = values[piece * STEP : (piece + 1) * STEP, :]


def laid(table, tile):
    starts = range(0, PARTS * APART, APART)
    return jnp.concatenate([table[tile, start : start + STEP, :] for start in starts])


def ends_of(signal, ends, keep, tile, flipped):
    decay = [spread(keep, tile, m) for m in range(MODES)]

    def step(i, states):
        at = STEP - 1 - i if flipped else i
        u = signal[tile, pl.ds(at, PARTS, stride=APART), :]
        return tuple(decay[m] * states[m] + u for m in range(MODES))

    zero = jnp.zeros((PARTS, LANES), F32)
    states = lax.fori_loop(0, STEP, step, (zero,) * MODES, unroll=16)
    for m in range(MODES):
        ends[tile, pl.ds(m, PARTS, stride=MODES), :] = states[m]


def chain(ends, starts, total, keep_piece, tile, flipped):
    state = jnp.zeros((MODES, LANES), F32)
    factor = keep_piece[tile]
    order = range(PARTS - 1, -1, -1) if flipped else range(PARTS)
    for piece in order:
        rows = slice(piece * MODES, (piece + 1) * MODES)
        starts[tile, rows, :] = state
        state = factor * state + ends[tile, rows, :]
    total[tile] = state


def whole_starts(starts, initial, begin, keep_piece, tile, flipped):
    carried = initial
    factor = keep_piece[tile]
    order = range(PARTS - 1, -1, -1) if flipped else range(PARTS)
    for piece in order:
        rows = slice(piece * MODES, (piece + 1) * MODES)
        begin[tile, rows, :] = starts[tile, rows, :] + carried
        carried = factor * carried


def responses(signal, begin, result, keep, gain, tile, flipped):
    decay = [spread(keep, tile, m) for m in range(MODES)]
    gains = [spread(gain, tile, m) for m in range(MODES)]

    def step(i, states):
        at = STEP - 1 - i if flipped else i
        u = signal[tile, pl.ds(at, PARTS, stride=APART), :]
        states = tuple(decay[m] * states[m] + u for m in range(MODES))
        terms = [gains[m] * states[m] for m in range(MODES)]
        while len(terms) > 1:
            terms = [terms[i] + terms[i + 1] for i in range(0, len(terms), 2)]
        result[tile, pl.ds(at, PARTS, stride=APART), :] = terms[0]
        return states

    states = tuple(begin[tile, pl.ds(m, PARTS, stride=MODES), :] for m in range(MODES))
    lax.fori_loop(0, STEP, step, states, unroll=16)


def dot(a, b):
    return jnp.dot(a, b, preferred_element_type=F32)


def turned(a, b):
    return lax.dot_general(a, b, (((1,), (1,)), ((), ())), preferred_element_type=F32)


def wide(value):
    return value.astype(F32)


NEAR = [(0, 0), (1, 0), (0, -1), (0, 1), (1, -1), (1, 1), (0, 2), (1, 2)]
OWN, ACROSS, BEHIND, AHEAD, ACROSS_BEHIND, ACROSS_AHEAD, FAR, ACROSS_FAR = range(8)
TOP, BOTTOM = slice(0, HALF), slice(HALF, ROWS)
FIRST, SECOND = slice(0, ROWS), slice(ROWS, 2 * ROWS)
PER_TILE = range(TILES)


def columns(weight, which):
    at, step = lax.axis_index("tp"), 1 - 2 * lax.rem(lax.axis_index("ctx"), 2)
    dx, dy = NEAR[which]
    x = lax.rem(lax.div(at, 4) + dx, 2)
    y = lax.rem(lax.rem(at, 4) + step * dy + 4, 4)
    return weight[:, pl.ds(pl.multiple_of((x * 4 + y) * COLS, COLS), COLS)]


def gate_kernel(
    gated, fading, amplitude, rates, keep, keep_piece, gain, starts, total, signal, ends,
):
    for tile in PER_TILE:
        at = tile_of(tile)
        rates[tile] = -fading[:, at]
        gain[tile] = amplitude[:, at]
        keep[tile] = jnp.exp(-rates[tile])
        keep_piece[tile] = jnp.exp(rates[tile] * -float(STEP))
        lay(signal, tile, wide(gated[:, at]))
        ends_of(signal, ends, keep, tile, False)
        chain(ends, starts, total, keep_piece, tile, False)


def power(rates, n):
    return jnp.exp(rates * (-float(ROWS) * jnp.asarray(n).astype(F32)))


def spot_of(flipped):
    line = lax.axis_index("ctx")
    core, high, z = lax.rem(line, 2), lax.rem(lax.div(line, 2), 2), lax.div(line, 4)
    return (1 - core, 1 - high, 7 - z) if flipped else (core, high, z)


def pair_kernel(flipped, rates, own, other, pair, before):
    core, _, _ = spot_of(flipped)
    pair[...] = power(rates[...], 1 - core) * own[...] + power(rates[...], core) * other[...]
    before[...] = core.astype(F32) * other[...]


def three_kernel(flipped, rates, pair, one_off, two_off, two, three):
    _, _, z = spot_of(flipped)
    here = (z >= 1).astype(F32) * one_off[...]
    here += (z >= 2).astype(F32) * (power(rates[...], 4) * two_off[...])
    two[...] = here
    three[...] = pair[...] + power(rates[...], 4) * here


def over_of(rates, z, two, three_off, six_off):
    here = two + (z >= 3).astype(F32) * (power(rates, 8) * three_off)
    return here + (z >= 6).astype(F32) * (power(rates, 20) * six_off)


def sent_kernel(flipped, rates, pair, two, three_off, six_off, after, after_too, over, sent):
    _, high, z = spot_of(flipped)
    here = over_of(rates[...], z, two[...], three_off[...], six_off[...])
    over[...] = here
    later = high.astype(F32)
    sent[...] = later * here + (1.0 - later) * (pair[...] + power(rates[...], 4) * here)


def group_kernel(flipped, rates, pair, before, other, group, before_all):
    core, high, _ = spot_of(flipped)
    early, late = power(rates[...], 2 - 2 * high), power(rates[...], 2 * high)
    group[...] = early * pair[...] + late * other[...]
    before_all[...] = before[...] + high.astype(F32) * (power(rates[...], core) * other[...])


def relay_kernel(across, behind, ahead, after, after_too, across_out, behind_out):
    across_out[...] = across[...]
    behind_out[...] = behind[...]


def mix_kernel(
    rates, other, over, before,
    gated, starts, keep, keep_piece, gain, skip, query, after,
    summed, mixed_in,
    signal, result, begin,
):
    for tile in PER_TILE:
        at = tile_of(tile)
        lay(signal, tile, wide(gated[:, at]))
        core, _, _ = spot_of(False)
        initial = other[tile] + power(rates[tile], 2) * over[tile]
        initial = power(rates[tile], core) * initial + before[tile]
        whole_starts(starts, initial, begin, keep_piece, tile, False)
        responses(signal, begin, result, keep, gain, tile, False)
        conv = wide(laid(result, tile).astype(BF16))
        total = conv + skip[0:1, at] * wide(gated[:, at])
        summed[:, at] = total
        mixed_in[:, at] = (wide(query[:, at]) * total).astype(BF16)


def products(mixed_in, weight, outs):
    for out, start, which in outs:
        for rows in (TOP, BOTTOM):
            part = dot(mixed_in[rows, :], columns(weight, which))
            out[start + rows.start : start + rows.stop, :] = part.astype(BF16)


def first_kernel(mixed_in, weight, across_far, far):
    products(mixed_in, weight, ((across_far, 0, ACROSS_FAR), (far, 0, FAR)))


def over_kernel(mixed_in, weight, after, over, side):
    products(mixed_in, weight, ((over, 0, ACROSS_BEHIND), (side, 0, ACROSS_AHEAD)))


def rest_kernel(mixed_in, weight, after, ahead, behind, across, own):
    outs = ((ahead, 0, AHEAD),)
    products(mixed_in, weight, outs + ((behind, 0, BEHIND), (across, 0, ACROSS), (own, 0, OWN)))


def sum_kernel(got, part, after, out):
    out[...] = (wide(part[...]) + wide(got[...])).astype(BF16)


def last_kernel(own, ahead, behind, across, out):
    inner = wide(own[...]) + wide(ahead[...])
    out[...] = (inner + (wide(behind[...]) + wide(across[...]))).astype(BF16)


def early_kernel(weight, own, across, behind, ahead, after, acc):
    blocks = ((own, OWN), (across, ACROSS), (behind, BEHIND), (ahead, AHEAD))
    for rows in (TOP, BOTTOM):
        grad = jnp.zeros((HALF, COLS), F32)
        for ref, which in blocks:
            grad += turned(ref[rows, :], columns(weight, which))
        acc[rows, :] = grad


def later_kernel(weight, acc, got_across, got_behind, over, total):
    parts = ((got_across, ACROSS_BEHIND), (got_behind, FAR), (over, ACROSS_AHEAD))
    for rows in (TOP, BOTTOM):
        grad = acc[rows, :]
        for ref, which in parts:
            grad += turned(ref[rows, :], columns(weight, which))
        total[rows, :] = grad


def grad_kernel(
    weight, acc, far, query, summed, keep, keep_piece, after,
    grad_query, grad_conv, starts, total,
    full, signal, ends,
):
    for rows in (TOP, BOTTOM):
        grad = acc[rows, :] + turned(far[rows, :], columns(weight, ACROSS_FAR))
        full[rows, :] = grad
    for tile in PER_TILE:
        at = tile_of(tile)
        grad_query[:, at] = (full[:, at] * summed[:, at]).astype(BF16)
        conv = (full[:, at] * wide(query[:, at])).astype(BF16)
        grad_conv[:, at] = conv
        lay(signal, tile, wide(conv))
        ends_of(signal, ends, keep, tile, True)
        chain(ends, starts, total, keep_piece, tile, True)


def back_kernel(
    rates, two, three_off, six_off, before,
    grad_conv, starts, keep, keep_piece, gain, skip, key, value,
    grad_key, grad_value,
    signal, result, begin,
):
    for tile in PER_TILE:
        at = tile_of(tile)
        lay(signal, tile, wide(grad_conv[:, at]))
        core, high, z = spot_of(True)
        over = over_of(rates[tile], z, two[tile], three_off[tile], six_off[tile])
        initial = power(rates[tile], 2 * high + core) * over + before[tile]
        whole_starts(starts, initial, begin, keep_piece, tile, True)
        responses(signal, begin, result, keep, gain, tile, True)
        back = wide(laid(result, tile).astype(BF16))
        total = back + skip[0:1, at] * wide(grad_conv[:, at])
        grad_key[:, at] = (total * wide(value[:, at])).astype(BF16)
        grad_value[:, at] = (total * wide(key[:, at])).astype(BF16)


STATE_SHAPE, BLOCK, TWICE = (TILES, MODES, LANES), (ROWS, COLS), (2 * ROWS, COLS)
TABLE, DEEP = (TILES, PARTS * MODES, LANES), (TILES, PARTS * APART, LANES)


def call(kernel, outs, scratch, micros, mib, *args):
    return pl.pallas_call(
        kernel,
        out_shape=[jax.ShapeDtypeStruct(shape, kind) for shape, kind in outs],
        in_specs=[VMEM] * len(args),
        out_specs=[VMEM] * len(outs),
        scratch_shapes=[pltpu.VMEM(shape, kind) for shape, kind in scratch],
        cost_estimate=pl.CostEstimate(
            flops=int(micros * 1.1e9), bytes_accessed=int(micros * 3e6), transcendentals=0
        ),
        compiler_params=pltpu.CompilerParams(vmem_limit_bytes=mib * 1024 * 1024),
    )(*args)


def ctx_perm(move):
    pairs = []
    for z in range(8):
        for h in range(2):
            for c in range(2):
                to = move(z, h, c)
                pairs.append((z * 4 + h * 2 + c, to[0] % 8 * 4 + to[1] % 2 * 2 + to[2] % 2))
    return pairs


def shift_x(value):
    return lax.ppermute(value, "tp", [(at, (at + 4) % 8) for at in range(8)])


def along_y(value, turn):
    pairs = []
    for line in range(32):
        step = turn * (1 - 2 * (line % 2))
        for at in range(8):
            pairs.append((line * 8 + at, line * 8 + at // 4 * 4 + (at + step) % 4))
    return lax.ppermute(value, ("ctx", "tp"), pairs)


def small(kernel, flipped, *args):
    both = [(STATE_SHAPE, F32)] * 2
    return call(functools.partial(kernel, flipped), both, [], 1.0, 4, *args)


def other_core(value):
    return lax.ppermute(value, "ctx", ctx_perm(lambda z, h, c: (z, h, c + 1)))


def other_half(value):
    return lax.ppermute(value, "ctx", ctx_perm(lambda z, h, c: (z, h + 1, c)))


def earlier(value, k, flipped):
    move = -k if flipped else k
    return lax.ppermute(value, "ctx", ctx_perm(lambda z, h, c: (z + move, h, c)))


def per_device(query, key, value, cotangent, weight, decay_rates, residues, skip_gain):
    decay_rates, residues = decay_rates.T, residues.T
    amplitude = residues * jnp.sqrt(-jnp.expm1(-2.0 * decay_rates))
    fading = -decay_rates
    skip = skip_gain.reshape(1, COLS)

    across = shift_x(cotangent)
    behind = along_y(cotangent, 1)
    ahead = along_y(cotangent, -1)

    deep, table, state = (DEEP, F32), (TABLE, F32), (STATE_SHAPE, F32)
    gated = (key.astype(F32) * value.astype(F32)).astype(BF16)
    rates, keep, keep_piece, gain, starts, total = call(
        gate_kernel, [state] * 4 + [table, state], [deep, table], 2.4, 6, gated, fading, amplitude
    )
    pair, before = small(pair_kernel, False, rates, total, other_core(total))
    offs = earlier(pair, 1, False), earlier(pair, 2, False)
    s_across, s_behind = call(
        relay_kernel, [(BLOCK, BF16)] * 2, [], 1.0, 4, across, behind, ahead, *offs
    )
    got_across, got_behind, over = along_y(s_across, 1), along_y(s_behind, 1), shift_x(ahead)
    far = along_y(got_across, 1)
    (acc,) = call(
        early_kernel,
        [(BLOCK, F32)],
        [],
        2.0,
        6,
        weight,
        cotangent,
        across,
        behind,
        ahead,
        s_across,
    )

    two, three = small(three_kernel, False, rates, pair, *offs)
    offs = earlier(three, 3, False), earlier(three, 6, False)
    over_state, sent = small(sent_kernel, False, rates, pair, two, *offs, acc, got_across)
    (acc,) = call(
        later_kernel, [(BLOCK, F32)], [], 1.5, 6, weight, acc, got_across, got_behind, over
    )
    carried = other_half(sent), over_state, before
    summed, mixed_in = call(
        mix_kernel,
        [(BLOCK, F32), (BLOCK, BF16)],
        [deep, deep, table],
        4.5,
        8,
        rates,
        *carried,
        gated,
        starts,
        keep,
        keep_piece,
        gain,
        skip,
        query,
        got_across,
    )
    s_across_far, s_along = call(
        first_kernel, [(BLOCK, BF16)] * 2, [], 1.0, 6, mixed_in, weight
    )
    g_across_far, g_along = along_y(s_across_far, 1), along_y(s_along, 1)
    grad_query, grad_conv, back_starts, back_total = call(
        grad_kernel,
        [(BLOCK, BF16), (BLOCK, BF16), table, state],
        [(BLOCK, F32), deep, table],
        6.0,
        8,
        weight,
        acc,
        far,
        query,
        summed,
        keep,
        keep_piece,
        s_along,
    )
    pair, before = small(pair_kernel, True, rates, back_total, other_core(back_total))
    half_other = other_half(pair)
    s_over, side = call(over_kernel, [(BLOCK, BF16)] * 2, [], 0.7, 6, mixed_in, weight, pair)
    group, before = small(group_kernel, True, rates, pair, before, half_other)
    ahead_part, behind_part, across_part, own_part = call(
        rest_kernel, [(BLOCK, BF16)] * 4, [], 2.0, 6, mixed_in, weight, group
    )
    offs = earlier(group, 1, True), earlier(group, 2, True)
    two, three = small(three_kernel, True, rates, group, *offs)
    offs = earlier(three, 3, True), earlier(three, 6, True)

    g_over = shift_x(s_over)
    (s_side,) = call(sum_kernel, [(BLOCK, BF16)], [], 0.5, 4, g_across_far, side, group)
    (s_ahead,) = call(sum_kernel, [(BLOCK, BF16)], [], 0.5, 4, g_along, ahead_part, three)
    (s_behind,) = call(sum_kernel, [(BLOCK, BF16)], [], 0.5, 4, g_over, behind_part, three)
    g_side, g_ahead, g_behind = along_y(s_side, 1), along_y(s_ahead, 1), along_y(s_behind, -1)
    (s_across,) = call(sum_kernel, [(BLOCK, BF16)], [], 0.5, 4, g_side, across_part, three)
    (mixed,) = call(
        last_kernel, [(BLOCK, BF16)], [], 0.5, 4, own_part, g_ahead, g_behind, shift_x(s_across)
    )
    grad_key, grad_value = call(
        back_kernel,
        [(BLOCK, BF16)] * 2,
        [deep, deep, table],
        4.5,
        8,
        rates,
        two,
        *offs,
        before,
        grad_conv,
        back_starts,
        keep,
        keep_piece,
        gain,
        skip,
        key,
        value,
    )
    return mixed, grad_query, grad_key, grad_value


def solution(mesh):
    split, rows = P("ctx", "tp"), P("tp", None)
    return jax.shard_map(
        per_device,
        mesh=mesh,
        in_specs=(split, split, split, split, rows, rows, rows, P("tp")),
        out_specs=(split, split, split, split),
        check_vma=False,
    )
```

```python
import functools

import jax
import jax.numpy as jnp
from jax import lax
from jax.experimental import pallas as pl
from jax.experimental.pallas import tpu as pltpu
from jax.sharding import PartitionSpec as P

F32, BF16 = jnp.float32, jnp.bfloat16
ROWS, COLS, MODES, LANES = 512, 512, 16, 128
HALF = ROWS // 2
TILES = COLS // LANES
PARTS = 8
STEP = ROWS // PARTS
APART = STEP + 8
VMEM = pl.BlockSpec(memory_space=pltpu.VMEM)


def tile_of(tile):
    return slice(tile * LANES, (tile + 1) * LANES)


def spread(ref, tile, mode):
    return jnp.broadcast_to(ref[tile, mode : mode + 1, :], (PARTS, LANES))


def lay(table, tile, values):
    for piece in range(PARTS):
        rows = slice(piece * APART, piece * APART + STEP)
        table[tile, rows, :] = values[piece * STEP : (piece + 1) * STEP, :]


def laid(table, tile):
    starts = range(0, PARTS * APART, APART)
    return jnp.concatenate([table[tile, start : start + STEP, :] for start in starts])


def ends_of(signal, ends, keep, tile, flipped):
    decay = [spread(keep, tile, m) for m in range(MODES)]

    def step(i, states):
        at = STEP - 1 - i if flipped else i
        u = signal[tile, pl.ds(at, PARTS, stride=APART), :]
        return tuple(decay[m] * states[m] + u for m in range(MODES))

    zero = jnp.zeros((PARTS, LANES), F32)
    states = lax.fori_loop(0, STEP, step, (zero,) * MODES, unroll=16)
    for m in range(MODES):
        ends[tile, pl.ds(m, PARTS, stride=MODES), :] = states[m]


def chain(ends, starts, total, keep_piece, tile, flipped):
    state = jnp.zeros((MODES, LANES), F32)
    factor = keep_piece[tile]
    order = range(PARTS - 1, -1, -1) if flipped else range(PARTS)
    for piece in order:
        rows = slice(piece * MODES, (piece + 1) * MODES)
        starts[tile, rows, :] = state
        state = factor * state + ends[tile, rows, :]
    total[tile] = state


def whole_starts(starts, initial, begin, keep_piece, tile, flipped):
    carried = initial
    factor = keep_piece[tile]
    order = range(PARTS - 1, -1, -1) if flipped else range(PARTS)
    for piece in order:
        rows = slice(piece * MODES, (piece + 1) * MODES)
        begin[tile, rows, :] = starts[tile, rows, :] + carried
        carried = factor * carried


def responses(signal, begin, result, keep, gain, tile, flipped):
    decay = [spread(keep, tile, m) for m in range(MODES)]
    gains = [spread(gain, tile, m) for m in range(MODES)]

    def step(i, states):
        at = STEP - 1 - i if flipped else i
        u = signal[tile, pl.ds(at, PARTS, stride=APART), :]
        states = tuple(decay[m] * states[m] + u for m in range(MODES))
        terms = [gains[m] * states[m] for m in range(MODES)]
        while len(terms) > 1:
            terms = [terms[i] + terms[i + 1] for i in range(0, len(terms), 2)]
        result[tile, pl.ds(at, PARTS, stride=APART), :] = terms[0]
        return states

    states = tuple(begin[tile, pl.ds(m, PARTS, stride=MODES), :] for m in range(MODES))
    lax.fori_loop(0, STEP, step, states, unroll=16)


def dot(a, b):
    return jnp.dot(a, b, preferred_element_type=F32)


def turned(a, b):
    return lax.dot_general(a, b, (((1,), (1,)), ((), ())), preferred_element_type=F32)


def wide(value):
    return value.astype(F32)


NEAR = [(0, 0), (1, 0), (0, -1), (0, 1), (1, -1), (1, 1), (0, 2), (1, 2)]
OWN, ACROSS, BEHIND, AHEAD, ACROSS_BEHIND, ACROSS_AHEAD, FAR, ACROSS_FAR = range(8)
TOP, BOTTOM = slice(0, HALF), slice(HALF, ROWS)
FIRST, SECOND = slice(0, ROWS), slice(ROWS, 2 * ROWS)
PER_TILE = range(TILES)


def columns(weight, which):
    at, step = lax.axis_index("tp"), 1 - 2 * lax.rem(lax.axis_index("ctx"), 2)
    dx, dy = NEAR[which]
    x = lax.rem(lax.div(at, 4) + dx, 2)
    y = lax.rem(lax.rem(at, 4) + step * dy + 4, 4)
    return weight[:, pl.ds(pl.multiple_of((x * 4 + y) * COLS, COLS), COLS)]


def gate_kernel(
    gated, fading, amplitude, rates, keep, keep_piece, gain, starts, total, signal, ends,
):
    for tile in PER_TILE:
        at = tile_of(tile)
        rates[tile] = -fading[:, at]
        gain[tile] = amplitude[:, at]
        keep[tile] = jnp.exp(-rates[tile])
        keep_piece[tile] = jnp.exp(rates[tile] * -float(STEP))
        lay(signal, tile, wide(gated[:, at]))
        ends_of(signal, ends, keep, tile, False)
        chain(ends, starts, total, keep_piece, tile, False)


def power(rates, n):
    return jnp.exp(rates * (-float(ROWS) * jnp.asarray(n).astype(F32)))


def spot_of(flipped):
    line = lax.axis_index("ctx")
    core, high, z = lax.rem(line, 2), lax.rem(lax.div(line, 2), 2), lax.div(line, 4)
    return (1 - core, 1 - high, 7 - z) if flipped else (core, high, z)


def pair_kernel(flipped, rates, own, other, pair, before):
    core, _, _ = spot_of(flipped)
    pair[...] = power(rates[...], 1 - core) * own[...] + power(rates[...], core) * other[...]
    before[...] = core.astype(F32) * other[...]


def three_kernel(flipped, rates, pair, one_off, two_off, two, three):
    _, _, z = spot_of(flipped)
    here = (z >= 1).astype(F32) * one_off[...]
    here += (z >= 2).astype(F32) * (power(rates[...], 4) * two_off[...])
    two[...] = here
    three[...] = pair[...] + power(rates[...], 4) * here


def over_of(rates, z, two, three_off, six_off):
    here = two + (z >= 3).astype(F32) * (power(rates, 8) * three_off)
    return here + (z >= 6).astype(F32) * (power(rates, 20) * six_off)


def sent_kernel(flipped, rates, pair, two, three_off, six_off, after, after_too, over, sent):
    _, high, z = spot_of(flipped)
    here = over_of(rates[...], z, two[...], three_off[...], six_off[...])
    over[...] = here
    later = high.astype(F32)
    sent[...] = later * here + (1.0 - later) * (pair[...] + power(rates[...], 4) * here)


def group_kernel(flipped, rates, pair, before, other, group, before_all):
    core, high, _ = spot_of(flipped)
    early, late = power(rates[...], 2 - 2 * high), power(rates[...], 2 * high)
    group[...] = early * pair[...] + late * other[...]
    before_all[...] = before[...] + high.astype(F32) * (power(rates[...], core) * other[...])


def relay_kernel(across, behind, ahead, after, after_too, across_out, behind_out):
    across_out[...] = across[...]
    behind_out[...] = behind[...]


def mix_kernel(
    rates, other, over, before,
    gated, starts, keep, keep_piece, gain, skip, query, after,
    summed, mixed_in,
    signal, result, begin,
):
    for tile in PER_TILE:
        at = tile_of(tile)
        lay(signal, tile, wide(gated[:, at]))
        core, _, _ = spot_of(False)
        initial = other[tile] + power(rates[tile], 2) * over[tile]
        initial = power(rates[tile], core) * initial + before[tile]
        whole_starts(starts, initial, begin, keep_piece, tile, False)
        responses(signal, begin, result, keep, gain, tile, False)
        conv = wide(laid(result, tile).astype(BF16))
        total = conv + skip[0:1, at] * wide(gated[:, at])
        summed[:, at] = total
        mixed_in[:, at] = (wide(query[:, at]) * total).astype(BF16)


def products(mixed_in, weight, outs):
    for out, start, which in outs:
        for rows in (TOP, BOTTOM):
            part = dot(mixed_in[rows, :], columns(weight, which))
            out[start + rows.start : start + rows.stop, :] = part.astype(BF16)


def first_kernel(mixed_in, weight, across_far, far):
    products(mixed_in, weight, ((across_far, 0, ACROSS_FAR), (far, 0, FAR)))


def over_kernel(mixed_in, weight, after, over, side):
    products(mixed_in, weight, ((over, 0, ACROSS_BEHIND), (side, 0, ACROSS_AHEAD)))


def rest_kernel(mixed_in, weight, after, ahead, behind, across, own):
    outs = ((ahead, 0, AHEAD),)
    products(mixed_in, weight, outs + ((behind, 0, BEHIND), (across, 0, ACROSS), (own, 0, OWN)))


def sum_kernel(got, part, after, out):
    out[...] = (wide(part[...]) + wide(got[...])).astype(BF16)


def last_kernel(own, ahead, behind, across, out):
    inner = wide(own[...]) + wide(ahead[...])
    out[...] = (inner + (wide(behind[...]) + wide(across[...]))).astype(BF16)


def early_kernel(weight, own, across, behind, ahead, after, acc):
    blocks = ((own, OWN), (across, ACROSS), (behind, BEHIND), (ahead, AHEAD))
    for rows in (TOP, BOTTOM):
        grad = jnp.zeros((HALF, COLS), F32)
        for ref, which in blocks:
            grad += turned(ref[rows, :], columns(weight, which))
        acc[rows, :] = grad


def later_kernel(weight, acc, got_across, got_behind, over, total):
    parts = ((got_across, ACROSS_BEHIND), (got_behind, FAR), (over, ACROSS_AHEAD))
    for rows in (TOP, BOTTOM):
        grad = acc[rows, :]
        for ref, which in parts:
            grad += turned(ref[rows, :], columns(weight, which))
        total[rows, :] = grad


def grad_kernel(
    weight, acc, far, query, summed, keep, keep_piece, after,
    grad_query, grad_conv, starts, total,
    full, signal, ends,
):
    for rows in (TOP, BOTTOM):
        grad = acc[rows, :] + turned(far[rows, :], columns(weight, ACROSS_FAR))
        full[rows, :] = grad
    for tile in PER_TILE:
        at = tile_of(tile)
        grad_query[:, at] = (full[:, at] * summed[:, at]).astype(BF16)
        conv = (full[:, at] * wide(query[:, at])).astype(BF16)
        grad_conv[:, at] = conv
        lay(signal, tile, wide(conv))
        ends_of(signal, ends, keep, tile, True)
        chain(ends, starts, total, keep_piece, tile, True)


def back_kernel(
    rates, two, three_off, six_off, before,
    grad_conv, starts, keep, keep_piece, gain, skip, key, value,
    grad_key, grad_value,
    signal, result, begin,
):
    for tile in PER_TILE:
        at = tile_of(tile)
        lay(signal, tile, wide(grad_conv[:, at]))
        core, high, z = spot_of(True)
        over = over_of(rates[tile], z, two[tile], three_off[tile], six_off[tile])
        initial = power(rates[tile], 2 * high + core) * over + before[tile]
        whole_starts(starts, initial, begin, keep_piece, tile, True)
        responses(signal, begin, result, keep, gain, tile, True)
        back = wide(laid(result, tile).astype(BF16))
        total = back + skip[0:1, at] * wide(grad_conv[:, at])
        grad_key[:, at] = (total * wide(value[:, at])).astype(BF16)
        grad_value[:, at] = (total * wide(key[:, at])).astype(BF16)


STATE_SHAPE, BLOCK, TWICE = (TILES, MODES, LANES), (ROWS, COLS), (2 * ROWS, COLS)
TABLE, DEEP = (TILES, PARTS * MODES, LANES), (TILES, PARTS * APART, LANES)


def call(kernel, outs, scratch, micros, mib, *args):
    return pl.pallas_call(
        kernel,
        out_shape=[jax.ShapeDtypeStruct(shape, kind) for shape, kind in outs],
        in_specs=[VMEM] * len(args),
        out_specs=[VMEM] * len(outs),
        scratch_shapes=[pltpu.VMEM(shape, kind) for shape, kind in scratch],
        cost_estimate=pl.CostEstimate(
            flops=int(micros * 1.1e9), bytes_accessed=int(micros * 3e6), transcendentals=0
        ),
        compiler_params=pltpu.CompilerParams(vmem_limit_bytes=mib * 1024 * 1024),
    )(*args)


def ctx_perm(move):
    pairs = []
    for z in range(8):
        for h in range(2):
            for c in range(2):
                to = move(z, h, c)
                pairs.append((z * 4 + h * 2 + c, to[0] % 8 * 4 + to[1] % 2 * 2 + to[2] % 2))
    return pairs


def shift_x(value):
    return lax.ppermute(value, "tp", [(at, (at + 4) % 8) for at in range(8)])


def along_y(value, turn):
    pairs = []
    for line in range(32):
        step = turn * (1 - 2 * (line % 2))
        for at in range(8):
            pairs.append((line * 8 + at, line * 8 + at // 4 * 4 + (at + step) % 4))
    return lax.ppermute(value, ("ctx", "tp"), pairs)


def small(kernel, flipped, *args):
    both = [(STATE_SHAPE, F32)] * 2
    return call(functools.partial(kernel, flipped), both, [], 1.0, 4, *args)


def other_core(value):
    return lax.ppermute(value, "ctx", ctx_perm(lambda z, h, c: (z, h, c + 1)))


def other_half(value):
    return lax.ppermute(value, "ctx", ctx_perm(lambda z, h, c: (z, h + 1, c)))


def earlier(value, k, flipped):
    move = -k if flipped else k
    return lax.ppermute(value, "ctx", ctx_perm(lambda z, h, c: (z + move, h, c)))


def per_device(query, key, value, cotangent, weight, decay_rates, residues, skip_gain):
    decay_rates, residues = decay_rates.T, residues.T
    amplitude = residues * jnp.sqrt(-jnp.expm1(-2.0 * decay_rates))
    fading = -decay_rates
    skip = skip_gain.reshape(1, COLS)

    across = shift_x(cotangent)
    behind = along_y(cotangent, 1)

    deep, table, state = (DEEP, F32), (TABLE, F32), (STATE_SHAPE, F32)
    gated = (key.astype(F32) * value.astype(F32)).astype(BF16)
    rates, keep, keep_piece, gain, starts, total = call(
        gate_kernel, [state] * 4 + [table, state], [deep, table], 2.4, 6, gated, fading, amplitude
    )
    pair, before = small(pair_kernel, False, rates, total, other_core(total))
    late, _ = lax.optimization_barrier((cotangent, pair))
    ahead = along_y(late, -1)
    offs = earlier(pair, 1, False), earlier(pair, 2, False)
    s_across, s_behind = call(
        relay_kernel, [(BLOCK, BF16)] * 2, [], 1.0, 4, across, behind, ahead, *offs
    )
    got_across, got_behind, over = along_y(s_across, 1), along_y(s_behind, 1), shift_x(ahead)
    far = along_y(got_across, 1)
    (acc,) = call(
        early_kernel,
        [(BLOCK, F32)],
        [],
        2.0,
        6,
        weight,
        cotangent,
        across,
        behind,
        ahead,
        s_across,
    )

    two, three = small(three_kernel, False, rates, pair, *offs)
    offs = earlier(three, 3, False), earlier(three, 6, False)
    over_state, sent = small(sent_kernel, False, rates, pair, two, *offs, acc, got_across)
    (acc,) = call(
        later_kernel, [(BLOCK, F32)], [], 1.5, 6, weight, acc, got_across, got_behind, over
    )
    carried = other_half(sent), over_state, before
    summed, mixed_in = call(
        mix_kernel,
        [(BLOCK, F32), (BLOCK, BF16)],
        [deep, deep, table],
        4.5,
        8,
        rates,
        *carried,
        gated,
        starts,
        keep,
        keep_piece,
        gain,
        skip,
        query,
        got_across,
    )
    s_across_far, s_along = call(
        first_kernel, [(BLOCK, BF16)] * 2, [], 1.0, 6, mixed_in, weight
    )
    g_across_far, g_along = along_y(s_across_far, 1), along_y(s_along, 1)
    grad_query, grad_conv, back_starts, back_total = call(
        grad_kernel,
        [(BLOCK, BF16), (BLOCK, BF16), table, state],
        [(BLOCK, F32), deep, table],
        6.0,
        8,
        weight,
        acc,
        far,
        query,
        summed,
        keep,
        keep_piece,
        s_along,
    )
    pair, before = small(pair_kernel, True, rates, back_total, other_core(back_total))
    half_other = other_half(pair)
    s_over, side = call(over_kernel, [(BLOCK, BF16)] * 2, [], 0.7, 6, mixed_in, weight, pair)
    group, before = small(group_kernel, True, rates, pair, before, half_other)
    ahead_part, behind_part, across_part, own_part = call(
        rest_kernel, [(BLOCK, BF16)] * 4, [], 2.0, 6, mixed_in, weight, group
    )
    offs = earlier(group, 1, True), earlier(group, 2, True)
    two, three = small(three_kernel, True, rates, group, *offs)
    offs = earlier(three, 3, True), earlier(three, 6, True)

    g_over = shift_x(s_over)
    (s_side,) = call(sum_kernel, [(BLOCK, BF16)], [], 0.5, 4, g_across_far, side, group)
    (s_ahead,) = call(sum_kernel, [(BLOCK, BF16)], [], 0.5, 4, g_along, ahead_part, three)
    (s_behind,) = call(sum_kernel, [(BLOCK, BF16)], [], 0.5, 4, g_over, behind_part, three)
    g_side, g_ahead, g_behind = along_y(s_side, 1), along_y(s_ahead, 1), along_y(s_behind, -1)
    (s_across,) = call(sum_kernel, [(BLOCK, BF16)], [], 0.5, 4, g_side, across_part, three)
    (mixed,) = call(
        last_kernel, [(BLOCK, BF16)], [], 0.5, 4, own_part, g_ahead, g_behind, shift_x(s_across)
    )
    grad_key, grad_value = call(
        back_kernel,
        [(BLOCK, BF16)] * 2,
        [deep, deep, table],
        4.5,
        8,
        rates,
        two,
        *offs,
        before,
        grad_conv,
        back_starts,
        keep,
        keep_piece,
        gain,
        skip,
        key,
        value,
    )
    return mixed, grad_query, grad_key, grad_value


def solution(mesh):
    split, rows = P("ctx", "tp"), P("tp", None)
    return jax.shard_map(
        per_device,
        mesh=mesh,
        in_specs=(split, split, split, split, rows, rows, rows, P("tp")),
        out_specs=(split, split, split, split),
        check_vma=False,
    )
```
